512 devices in a mesh: gx: 64 (over z, y), gy: 8 (over x, core).
Axes of the slice: x: 4, y: 4, z: 16, core: 2. Of those that a mesh axis runs over, the one named last changes fastest.
Arguments:
- tensor: bfloat16 [4096, 64, 4096], P('gx', None, 'gy'), may hold values from -104 to 104
- factor_b: bfloat16 [4096, 256], P('gy'), may hold values from -0.09375 to 0.09375
- factor_c: bfloat16 [64, 256], replicated, may hold values from -0.75 to 0.75
Outputs:
- a_hat: float32 [4096, 256], P('gx')
- b_hat: float32 [4096, 256], P('gy')
The draws below stay inside these ranges and needn't reach their ends.
All inputs are finite; a program needn't handle non-finite values.
Results may differ from the reference program's by a relative error of at most 0.0019.
The reference program's roundings to bfloat16 on the way (of `khatri_rao`) count: a program that leaves them out, or rounds other values in their place, can miss the bound.
Values sent between devices are 32-bit elements; how exact they have to be, the bound alone decides.
No kernel may reach another device: no remote copies, remote signals or barrier semaphores. Data moves between devices by JAX's collectives and lax.ppermute only.
A program may use at most 64 MiB of HBM per device.

```python
import math
import jax
import jax.numpy as jnp
from jax import lax

IX_DEV = 64
K = 64
R = 256
I = 4096
J = 4096
N_GX = 64


def draw_tensor(key, part):
    key = jax.random.fold_in(key, 11)
    key_base, key_rows, key_cols = jax.random.split(key, 3)
    position = jnp.arange(I, dtype=jnp.float32) / I
    row_scale = jnp.exp(math.log(3.0) * (position - 0.5) + jax.random.uniform(key_rows, (I,), jnp.float32, math.log(0.3), math.log(3.0)))
    col_scale = jnp.exp(jax.random.uniform(key_cols, (J,), jnp.float32, math.log(0.4), math.log(4.0)))
    base = jnp.clip(jax.random.normal(key_base, (I, K, J), jnp.float32), -5.0, 5.0)
    return (base * row_scale[:, None, None] * col_scale[None, None, :]).astype(jnp.bfloat16)


def shard_levels(stream_key, dims, shards, least, high):
    def one(dim, blocks):
        heights = jax.random.uniform(jax.random.fold_in(jax.random.fold_in(stream_key, 6), dim), (blocks,), jnp.float32, least / len(shards), high / len(shards))
        return jnp.repeat(jnp.exp(heights), dims[dim] // blocks).reshape((-1,) + (1,) * (len(dims) - dim - 1))

    factor_of = one(*shards[0])
    for cut in shards[1:]:
        factor_of = factor_of * one(*cut)
    return factor_of


def bell_draw(rng, dims, scale, reach, shards=(), kind=jnp.bfloat16):
    gain = shard_levels(rng, dims, shards, -0.22, 0.18) if shards else 1.0
    values = jax.random.normal(rng, dims, jnp.float32) * scale * gain
    return jnp.minimum(jnp.maximum(values, -reach), reach).astype(kind)


def setup_inputs(seed: int = 0) -> dict:
    key_list = jax.random.split(jax.random.key(seed), 4)
    tensor = draw_tensor(jax.random.fold_in(key_list[3], 71), 0)
    factor_b = bell_draw(key_list[1], (J, R), J ** -0.5, 0.09375, ((0, 8),))
    factor_c = bell_draw(key_list[2], (K, R), K ** -0.5, 0.75)
    return dict(tensor=tensor, factor_b=factor_b, factor_c=factor_c)


EPSILON = 1e-06

def lower_inverse(symmetric):
    order = symmetric.shape[0]
    if order == 1:
        return 1.0 / jnp.sqrt(symmetric)
    half = order // 2
    w_top = lower_inverse(symmetric[:half, :half])
    l_low = jnp.dot(symmetric[half:, :half], w_top.T, precision=lax.Precision.HIGHEST)
    schur = symmetric[half:, half:] - jnp.dot(l_low, l_low.T, precision=lax.Precision.HIGHEST)
    w_bottom = lower_inverse(schur)
    w_middle = -jnp.dot(w_bottom, jnp.dot(l_low, w_top, precision=lax.Precision.HIGHEST), precision=lax.Precision.HIGHEST)
    upper_band = jnp.concatenate([w_top, jnp.zeros((half, order - half), symmetric.dtype)], axis=1)
    lower_band = jnp.concatenate([w_middle, w_bottom], axis=1)
    return jnp.concatenate([upper_band, lower_band], axis=0)

def solve_rows(gram_matrix, right_rows):
    inverse_factor = lower_inverse(gram_matrix)
    halfway = jnp.dot(right_rows, inverse_factor.T, precision=lax.Precision.HIGHEST)
    return jnp.dot(halfway, inverse_factor, precision=lax.Precision.HIGHEST)

def reference(tensor, factor_b, factor_c):
    c_wide = factor_c.astype(jnp.float32)
    c_gram = jnp.dot(factor_c.T, factor_c, preferred_element_type=jnp.float32)
    b_gram = jnp.dot(factor_b.T, factor_b, preferred_element_type=jnp.float32)
    slabs = tensor.reshape(N_GX, IX_DEV, K, J)

    def first_mode(slab_rows):
        contracted = jnp.dot(slab_rows.reshape(IX_DEV * K, J), factor_b, preferred_element_type=jnp.float32)
        contracted = contracted.reshape(IX_DEV, K, R)
        return lax.optimization_barrier(jnp.sum(contracted * c_wide[None], axis=1))
    m_first = lax.map(first_mode, slabs).reshape(I, R)
    a_hat = solve_rows(b_gram * c_gram, m_first)
    col_squares = lax.optimization_barrier(jnp.sum(a_hat * a_hat, axis=0))
    a_unit = a_hat / jnp.sqrt(col_squares + EPSILON)
    a_gram = jnp.dot(a_unit.T, a_unit, precision=lax.Precision.HIGHEST)

    def second_mode(running, paired):
        slab_rows, a_rows = paired
        khatri_rao = (a_rows[:, None, :] * c_wide[None]).astype(jnp.bfloat16).reshape(IX_DEV * K, R)
        product = lax.dot_general(slab_rows.reshape(IX_DEV * K, J), khatri_rao, (((0,), (0,)), ((), ())), preferred_element_type=jnp.float32)
        return (running + product, None)
    m_second, unused = lax.scan(second_mode, jnp.zeros((J, R), jnp.float32), (slabs, a_unit.reshape(N_GX, IX_DEV, R)))
    b_hat = solve_rows(a_gram * c_gram, m_second)
    return (a_hat, b_hat)
```

```python
import functools

import jax
import jax.numpy as jnp
from jax import lax
from jax.experimental import pallas as pl
from jax.experimental.pallas import tpu as pltpu
from jax.sharding import Mesh
from jax.sharding import PartitionSpec as P

EPSILON = 1e-06
HIGH = lax.Precision.HIGHEST
BLOCK = 64
GROUP = 8
LANES = 128
PARTS = 8
STEPS = 12
RESIDUAL = 1e-8
VMEM_BYTES = 24 * 1024 * 1024
STREAM_BYTES = 115 * 512 * 1024
INVERSE_COST = pl.CostEstimate(flops=12_000_000_000, bytes_accessed=1_000_000, transcendentals=0)


def dot_nn(left, right):
    return lax.dot_general(left, right, (((1,), (0,)), ((), ())), precision=HIGH, preferred_element_type=jnp.float32)


def dot_tn(left, right):
    return lax.dot_general(left, right, (((0,), (0,)), ((), ())), precision=HIGH, preferred_element_type=jnp.float32)


def bf16_gram(factor):
    return lax.dot_general(factor, factor, (((0,), (0,)), ((), ())), preferred_element_type=jnp.float32)


def total(terms):
    terms = list(terms)
    while len(terms) > 1:
        paired = [terms[i] + terms[i + 1] for i in range(0, len(terms) - 1, 2)]
        terms = paired + ([terms[-1]] if len(terms) % 2 else [])
    return terms[0]


def solve_group(entries, rows):
    n = len(rows)
    e = [list(line) for line in entries]
    rows = list(rows)
    factors, scaled = {}, [None] * n
    for p in range(0, n, 2):
        a, b, c = e[p][p], e[p][p + 1], e[p + 1][p + 1]
        inv_det = pltpu.reciprocal(a * c - b * b, approx=True)
        inv_a, inv_b, inv_c = c * inv_det, b * inv_det, a * inv_det
        for i in range(p + 2, n):
            x, y = e[p][i], e[p + 1][i]
            f0, f1 = inv_a * x - inv_b * y, inv_c * y - inv_b * x
            factors[p, i] = f0, f1
            for j in range(i, n):
                e[i][j] = e[i][j] - (f0 * e[p][j] + f1 * e[p + 1][j])
            rows[i] = rows[i] - (f0 * rows[p] + f1 * rows[p + 1])
        scaled[p] = inv_a * rows[p] - inv_b * rows[p + 1]
        scaled[p + 1] = inv_c * rows[p + 1] - inv_b * rows[p]
    for p in range(n - 4, -1, -2):
        for q in range(2):
            scaled[p + q] = scaled[p + q] - total(factors[p, i][q] * scaled[i] for i in range(p + 2, n))
    return scaled


def block_inverse(block):
    order = block.shape[0]
    width = 2 * order
    count = order // GROUP
    eye = (
        lax.broadcasted_iota(jnp.int32, (order, order), 0) == lax.broadcasted_iota(jnp.int32, (order, order), 1)
    ).astype(jnp.float32)
    wide = jnp.concatenate([block, eye], axis=1)
    groups = [wide[g * GROUP : (g + 1) * GROUP] for g in range(count)]
    sub = lax.broadcasted_iota(jnp.int32, (GROUP, width), 0)
    full = (GROUP, width)
    for g in range(count):
        k = g * GROUP
        rows = [jnp.broadcast_to(groups[g][i : i + 1], full) for i in range(GROUP)]
        entries = [
            [jnp.broadcast_to(rows[i][:, k + j : k + j + 1], full) if j >= i else None for j in range(GROUP)]
            for i in range(GROUP)
        ]
        steps = solve_group(entries, rows)
        order_of = [h for h in range(g + 1, count)] + [h for h in range(g)]
        for h in order_of:
            cols = [jnp.broadcast_to(groups[h][:, k + j : k + j + 1], full) for j in range(GROUP)]
            groups[h] = groups[h] - total(cols[j] * steps[j] for j in range(GROUP))
        packed = steps[0]
        for i in range(1, GROUP):
            packed = jnp.where(sub == i, steps[i], packed)
        groups[g] = packed
    return jnp.concatenate([x[:, order:] for x in groups], axis=0)


def invert(work):
    order = work.shape[0]

    def sweep(_, carry):
        head = work[0:BLOCK, :]
        inv = block_inverse(head[:, 0:BLOCK])
        lane = lax.broadcasted_iota(jnp.int32, (BLOCK, order), 1)
        row = lax.broadcasted_iota(jnp.int32, (BLOCK, order), 0)
        band = dot_nn(inv, jnp.where(lane < BLOCK, (lane == row).astype(jnp.float32), head))
        rest = work[BLOCK:order, :]
        lane_low = lax.broadcasted_iota(jnp.int32, (order - BLOCK, order), 1)
        lower = jnp.where(lane_low < BLOCK, 0.0, rest) - dot_nn(rest[:, 0:BLOCK], band)
        work[0 : order - BLOCK, :] = pltpu.roll(lower, order - BLOCK, 1)
        work[order - BLOCK : order, :] = pltpu.roll(band, order - BLOCK, 1)
        return carry

    lax.fori_loop(0, order // BLOCK, sweep, 0)


def diagonal_mask(order):
    return lax.broadcasted_iota(jnp.int32, (order, order), 0) == lax.broadcasted_iota(jnp.int32, (order, order), 1)


def invert_scaled(matrix, work, inverse):
    order = matrix.shape[0]
    diagonal = diagonal_mask(order)
    kept = jnp.where(diagonal, matrix, 0.0)
    row = 1.0 / jnp.sqrt(jnp.sum(kept, axis=0, keepdims=True))
    col = 1.0 / jnp.sqrt(jnp.sum(kept, axis=1, keepdims=True))
    scaled = jnp.where(diagonal, 1.0, matrix * row * col)
    work[...] = scaled
    bound = jnp.max(jnp.sum(jnp.abs(scaled), axis=0, keepdims=True))
    size = jnp.where(bound < 2.0, 1.0, 1.0 / bound)
    inverse[...] = jnp.where(diagonal, 2.0 * size, 0.0) - (size * size) * scaled

    def unfinished(carry):
        residual, step = carry
        return (residual > RESIDUAL) & (step < STEPS)

    def improve(carry):
        step = carry[1]
        guess = inverse[...]
        error = jnp.where(diagonal_mask(order), 1.0, 0.0) - dot_nn(work[...], guess)
        inverse[...] = guess + dot_nn(guess, error)
        return jnp.sum(error * error), step + 1

    residual, _ = lax.while_loop(unfinished, improve, (jnp.float32(1.0), jnp.int32(0)))

    @pl.when(jnp.logical_not(residual <= RESIDUAL))
    def _():
        invert(work)
        inverse[...] = work[...]

    return row, col


def fetcher(source, kept, arrived):
    rows = source.shape[0] // PARTS

    def fetch(i):
        part = pl.ds(i * rows, rows)
        return pltpu.make_async_copy(source.at[part], kept.at[part], arrived.at[i])

    return fetch


def first_mode_kernel(tensor, factor_b, factor_c, out, kept, arrived):
    x_rows, time_len, depth = tensor.shape
    rank = factor_b.shape[1]
    rows, share = x_rows // PARTS, rank // PARTS

    fetch = fetcher(tensor, kept, arrived)
    for i in range(PARTS):
        fetch(i).start()
    gram = bf16_gram(factor_b[...])
    for i in range(PARTS):
        out[i, 0:share, :] = gram[i * share : (i + 1) * share]

    def contract(i, carry):
        fetch(i).wait()
        contracted = jnp.dot(
            kept[pl.ds(i * rows, rows)].reshape(rows * time_len, depth),
            factor_b[...],
            preferred_element_type=jnp.float32,
        ).reshape(rows, time_len, rank)
        out[i, share:, :] = jnp.sum(contracted * factor_c[...].astype(jnp.float32)[None], axis=1)
        return carry

    lax.fori_loop(0, PARTS, contract, 0)


def first_solve_kernel(where, gathered, factor_c, a_hat, slab, work, inverse, raw):
    rank = work.shape[0]
    share = rank // PARTS
    b_gram = jnp.concatenate([gathered[p, 0:share, :] for p in range(PARTS)], axis=0)
    m_first = jnp.concatenate([gathered[p, share:, :] for p in range(PARTS)], axis=0)
    row, _ = invert_scaled(b_gram * bf16_gram(factor_c[...]), work, inverse)
    rows = dot_nn(m_first * row, inverse[...]) * row
    a_hat[...] = rows
    raw[...] = dot_tn(rows, rows)
    mine = raw[pl.ds(where[0] * share, share), :]
    squares = jnp.sum(rows * rows, axis=0, keepdims=True)
    for p in range(PARTS):
        top, left = (p // 2) * GROUP, (p % 2) * LANES
        slab[p, 0:GROUP, :] = mine[top : top + GROUP, left : left + LANES]
        slab[p, GROUP:, :] = jnp.zeros((GROUP, LANES), jnp.float32)
        for h in range(rank // LANES):
            slab[p, GROUP + h : GROUP + h + 1, :] = squares[:, h * LANES : (h + 1) * LANES]


def assemble(pieces):
    bands = []
    for q in range(PARTS):
        for p in range(0, PARTS, 2):
            bands.append(jnp.concatenate([pieces[q, p], pieces[q, p + 1]], axis=1))
    return jnp.concatenate(bands, axis=0)


def norm_row(sums):
    squares = total(sums[p, GROUP:, :] for p in range(PARTS))
    return jnp.sqrt(jnp.concatenate([squares[0:1], squares[1:2]], axis=1) + EPSILON)


def second_mode_kernel(tensor, a_hat, sums, factor_c, out, kept, arrived):
    x_rows, time_len, depth = tensor.shape
    rank = a_hat.shape[1]
    rows, band = x_rows // PARTS, depth // PARTS
    fetch = fetcher(tensor, kept, arrived)
    for i in range(PARTS):
        fetch(i).start()
    norms = norm_row(sums)
    tile = total(sums[p, 0:GROUP, :] for p in range(PARTS))
    for p in range(PARTS):
        out[p, band:, 0:LANES] = tile
        out[p, band:, LANES:] = jnp.zeros((GROUP, rank - LANES), jnp.float32)
    out[:, 0:band, :] = jnp.zeros((PARTS, band, rank), jnp.float32)

    def contract(i, carry):
        fetch(i).wait()
        a_unit = a_hat[pl.ds(i * rows, rows), :] / norms
        khatri_rao = (a_unit[:, None, :] * factor_c[...].astype(jnp.float32)[None]).astype(jnp.bfloat16)
        out[:, 0:band, :] += lax.dot_general(
            kept[pl.ds(i * rows, rows)].reshape(rows * time_len, depth),
            khatri_rao.reshape(rows * time_len, rank),
            (((0,), (0,)), ((), ())),
            preferred_element_type=jnp.float32,
        ).reshape(PARTS, band, rank)
        return carry

    lax.fori_loop(0, PARTS, contract, 0)


def second_inverse_kernel(pieces, sums, factor_c, inverse, work):
    raw = assemble(pieces)
    norms = norm_row(sums)
    norms_down = jnp.sum(jnp.where(diagonal_mask(raw.shape[0]), norms, 0.0), axis=1, keepdims=True)
    row, col = invert_scaled(raw * bf16_gram(factor_c[...]), work, inverse)
    inverse[...] = inverse[...] * (row * norms) * (col * norms_down)


def second_solve_kernel(m_second, inverse, b_hat):
    b_hat[...] = dot_nn(total(m_second[p] for p in range(PARTS)), inverse[...])


def f32(*shape):
    return jax.ShapeDtypeStruct(shape, jnp.float32)


def call(kernel, out_shape, *operands, scratch=(), vmem=VMEM_BYTES, **more):
    return pl.pallas_call(
        kernel,
        out_shape=out_shape,
        scratch_shapes=list(scratch),
        compiler_params=pltpu.CompilerParams(vmem_limit_bytes=vmem),
        **more,
    )(*operands)


def scatter_sum(parts, axis):
    return jnp.sum(lax.all_to_all(parts, axis, 0, 0), axis=0)


def gather(block, axis):
    return lax.all_to_all(jnp.broadcast_to(block[None], (PARTS, *block.shape)), axis, 0, 0)


def local(tensor, factor_b, factor_c):
    x_rows, time_len, y_rows = tensor.shape
    rank = factor_b.shape[1]
    share = rank // PARTS
    x_step = x_rows // PARTS
    square = pltpu.VMEM((rank, rank), jnp.float32)

    whole = pl.BlockSpec(memory_space=pltpu.VMEM)
    streamed = dict(
        scratch=[pltpu.VMEM(tensor.shape, tensor.dtype), pltpu.SemaphoreType.DMA((PARTS,))], vmem=STREAM_BYTES
    )
    in_place = pl.BlockSpec(memory_space=pl.ANY)
    first = call(
        first_mode_kernel,
        f32(PARTS, share + x_step, rank),
        tensor,
        factor_b,
        factor_c,
        in_specs=[in_place, whole, whole],
        **streamed,
    )
    gathered = gather(scatter_sum(first, "gy"), "gy")

    where = lax.axis_index("gy").astype(jnp.int32).reshape(1)
    a_hat, slab = call(
        first_solve_kernel,
        (f32(x_rows, rank), f32(PARTS, 2 * GROUP, LANES)),
        where,
        gathered,
        factor_c,
        scratch=[square, square, square],
        in_specs=[pl.BlockSpec(memory_space=pltpu.SMEM), whole, whole],
    )

    sums = gather(scatter_sum(slab, "gl"), "gh")
    product = call(
        second_mode_kernel,
        f32(PARTS, y_rows // PARTS + GROUP, rank),
        tensor,
        a_hat,
        sums,
        factor_c,
        in_specs=[in_place, whole, whole, whole],
        **streamed,
    )
    received = lax.all_to_all(product, "gl", 0, 0)
    m_second = gather(jnp.sum(received[:, : y_rows // PARTS], axis=0), "gh")
    pieces = lax.all_gather(received[:, y_rows // PARTS :, :LANES], "gy")
    inverse = call(
        second_inverse_kernel, f32(rank, rank), pieces, sums, factor_c, scratch=[square], cost_estimate=INVERSE_COST
    )
    b_band = call(second_solve_kernel, f32(y_rows // PARTS, rank), m_second, inverse)
    b_hat = gather(b_band, "gl").reshape(y_rows, rank)
    return (a_hat, b_hat)


def solution(mesh):
    split = Mesh(mesh.devices.reshape(PARTS, PARTS, PARTS), ("gh", "gl", "gy"))
    x_axes = ("gh", "gl")
    return jax.shard_map(
        local,
        mesh=split,
        in_specs=(P(x_axes, None, "gy"), P("gy", None), P()),
        out_specs=(P(x_axes, None), P("gy", None)),
        check_vma=False,
    )
```

```python
import functools

import jax
import jax.numpy as jnp
from jax import lax
from jax.experimental import pallas as pl
from jax.experimental.pallas import tpu as pltpu
from jax.sharding import Mesh
from jax.sharding import PartitionSpec as P

EPSILON = 1e-06
HIGH = lax.Precision.HIGHEST
BLOCK = 64
GROUP = 8
LANES = 128
JOINED = 2
SLOTS = 5
PARTS = 8
STEPS = 12
RESIDUAL = 1e-8
VMEM_BYTES = 24 * 1024 * 1024
STREAM_BYTES = 115 * 512 * 1024
INVERSE_COST = pl.CostEstimate(flops=12_000_000_000, bytes_accessed=1_000_000, transcendentals=0)


def dot_nn(left, right):
    return lax.dot_general(left, right, (((1,), (0,)), ((), ())), precision=HIGH, preferred_element_type=jnp.float32)


def dot_tn(left, right):
    return lax.dot_general(left, right, (((0,), (0,)), ((), ())), precision=HIGH, preferred_element_type=jnp.float32)


def bf16_gram(factor):
    return lax.dot_general(factor, factor, (((0,), (0,)), ((), ())), preferred_element_type=jnp.float32)


def total(terms):
    terms = list(terms)
    while len(terms) > 1:
        paired = [terms[i] + terms[i + 1] for i in range(0, len(terms) - 1, 2)]
        terms = paired + ([terms[-1]] if len(terms) % 2 else [])
    return terms[0]


def solve_group(entries, rows):
    n = len(rows)
    e = [list(line) for line in entries]
    rows = list(rows)
    factors, scaled = {}, [None] * n
    for p in range(0, n, 2):
        a, b, c = e[p][p], e[p][p + 1], e[p + 1][p + 1]
        inv_det = pltpu.reciprocal(a * c - b * b, approx=True)
        inv_a, inv_b, inv_c = c * inv_det, b * inv_det, a * inv_det
        for i in range(p + 2, n):
            x, y = e[p][i], e[p + 1][i]
            f0, f1 = inv_a * x - inv_b * y, inv_c * y - inv_b * x
            factors[p, i] = f0, f1
            for j in range(i, n):
                e[i][j] = e[i][j] - (f0 * e[p][j] + f1 * e[p + 1][j])
            rows[i] = rows[i] - (f0 * rows[p] + f1 * rows[p + 1])
        scaled[p] = inv_a * rows[p] - inv_b * rows[p + 1]
        scaled[p + 1] = inv_c * rows[p + 1] - inv_b * rows[p]
    for p in range(n - 4, -1, -2):
        for q in range(2):
            scaled[p + q] = scaled[p + q] - total(factors[p, i][q] * scaled[i] for i in range(p + 2, n))
    return scaled


def block_inverse(block):
    order = block.shape[0]
    width = 2 * order
    count = order // GROUP
    eye = (
        lax.broadcasted_iota(jnp.int32, (order, order), 0) == lax.broadcasted_iota(jnp.int32, (order, order), 1)
    ).astype(jnp.float32)
    wide = jnp.concatenate([block, eye], axis=1)
    groups = [wide[g * GROUP : (g + 1) * GROUP] for g in range(count)]
    sub = lax.broadcasted_iota(jnp.int32, (GROUP, width), 0)
    full = (GROUP, width)
    for g in range(count):
        k = g * GROUP
        rows = [jnp.broadcast_to(groups[g][i : i + 1], full) for i in range(GROUP)]
        entries = [
            [jnp.broadcast_to(rows[i][:, k + j : k + j + 1], full) if j >= i else None for j in range(GROUP)]
            for i in range(GROUP)
        ]
        steps = solve_group(entries, rows)
        order_of = [h for h in range(g + 1, count)] + [h for h in range(g)]
        for h in order_of:
            cols = [jnp.broadcast_to(groups[h][:, k + j : k + j + 1], full) for j in range(GROUP)]
            groups[h] = groups[h] - total(cols[j] * steps[j] for j in range(GROUP))
        packed = steps[0]
        for i in range(1, GROUP):
            packed = jnp.where(sub == i, steps[i], packed)
        groups[g] = packed
    return jnp.concatenate([x[:, order:] for x in groups], axis=0)


def invert(work):
    order = work.shape[0]

    def sweep(_, carry):
        head = work[0:BLOCK, :]
        inv = block_inverse(head[:, 0:BLOCK])
        lane = lax.broadcasted_iota(jnp.int32, (BLOCK, order), 1)
        row = lax.broadcasted_iota(jnp.int32, (BLOCK, order), 0)
        band = dot_nn(inv, jnp.where(lane < BLOCK, (lane == row).astype(jnp.float32), head))
        rest = work[BLOCK:order, :]
        lane_low = lax.broadcasted_iota(jnp.int32, (order - BLOCK, order), 1)
        lower = jnp.where(lane_low < BLOCK, 0.0, rest) - dot_nn(rest[:, 0:BLOCK], band)
        work[0 : order - BLOCK, :] = pltpu.roll(lower, order - BLOCK, 1)
        work[order - BLOCK : order, :] = pltpu.roll(band, order - BLOCK, 1)
        return carry

    lax.fori_loop(0, order // BLOCK, sweep, 0)


def diagonal_mask(order):
    return lax.broadcasted_iota(jnp.int32, (order, order), 0) == lax.broadcasted_iota(jnp.int32, (order, order), 1)


def invert_scaled(matrix, work, inverse):
    order = matrix.shape[0]
    diagonal = diagonal_mask(order)
    kept = jnp.where(diagonal, matrix, 0.0)
    row = 1.0 / jnp.sqrt(jnp.sum(kept, axis=0, keepdims=True))
    col = 1.0 / jnp.sqrt(jnp.sum(kept, axis=1, keepdims=True))
    scaled = jnp.where(diagonal, 1.0, matrix * row * col)
    work[...] = scaled
    bound = jnp.max(jnp.sum(jnp.abs(scaled), axis=0, keepdims=True))
    size = jnp.where(bound < 2.0, 1.0, 1.0 / bound)
    inverse[...] = jnp.where(diagonal, 2.0 * size, 0.0) - (size * size) * scaled

    def unfinished(carry):
        residual, step = carry
        return (residual > RESIDUAL) & (step < STEPS)

    def improve(carry):
        step = carry[1]
        guess = inverse[...]
        error = jnp.where(diagonal_mask(order), 1.0, 0.0) - dot_nn(work[...], guess)
        inverse[...] = guess + dot_nn(guess, error)
        return jnp.sum(error * error), step + 1

    residual, _ = lax.while_loop(unfinished, improve, (jnp.float32(1.0), jnp.int32(0)))

    @pl.when(jnp.logical_not(residual <= RESIDUAL))
    def _():
        invert(work)
        inverse[...] = work[...]

    return row, col


def fetch_parts(source, kept, arrived):
    rows = source.shape[0] // PARTS

    def copy(i):
        part = pl.ds(i * rows, rows)
        return pltpu.make_async_copy(source.at[part], kept.at[part], arrived.at[i])

    for i in range(PARTS):
        copy(i).start()
    return lambda i: copy(i).wait()


def fetch_small(sources, targets, arrived):
    copies = [pltpu.make_async_copy(s, t, arrived.at[n]) for n, (s, t) in enumerate(zip(sources, targets))]
    for one in copies:
        one.start()
    return copies


def packed_gram(gram):
    low = lax.broadcasted_iota(jnp.int32, (BLOCK, LANES), 1) < BLOCK
    return [
        gram[0:64, 0:128],
        gram[128:192, 0:128],
        gram[192:256, 0:128],
        gram[192:256, 128:256],
        jnp.where(low, gram[128:192, 128:256], gram[64:128, 0:128]),
    ]


def unpacked_gram(slots):
    low = lax.broadcasted_iota(jnp.int32, (BLOCK, LANES), 1) < BLOCK
    none = jnp.zeros((BLOCK, LANES), jnp.float32)
    half = jnp.concatenate(
        [
            jnp.concatenate([slots[0], none], axis=1),
            jnp.concatenate([jnp.where(low, 0.0, slots[4]), none], axis=1),
            jnp.concatenate([slots[1], jnp.where(low, slots[4], 0.0)], axis=1),
            jnp.concatenate([slots[2], slots[3]], axis=1),
        ],
        axis=0,
    )
    shape = half.shape
    row_block = lax.broadcasted_iota(jnp.int32, shape, 0) // BLOCK
    col_block = lax.broadcasted_iota(jnp.int32, shape, 1) // BLOCK
    return half + jnp.where(row_block == col_block, 0.0, half).T


def first_mode_kernel(tensor_in, factor_b_in, factor_c_in, out, tensor, factor_b, factor_c, arrived, arrived_small):
    x_rows, time_len, depth = tensor.shape
    rank = factor_b.shape[1]
    rows = x_rows // PARTS
    small = fetch_small([factor_b_in, factor_c_in], [factor_b, factor_c], arrived_small)
    wait_part = fetch_parts(tensor_in, tensor, arrived)
    for one in small:
        one.wait()
    for t, slot in enumerate(packed_gram(bf16_gram(factor_b[...]))):
        for i in range(PARTS):
            out[i, t * GROUP : (t + 1) * GROUP, :] = slot[i * GROUP : (i + 1) * GROUP]

    def contract(i, carry):
        wait_part(i)
        contracted = jnp.dot(
            tensor[pl.ds(i * rows, rows)].reshape(rows * time_len, depth),
            factor_b[...],
            preferred_element_type=jnp.float32,
        ).reshape(rows, time_len, rank)
        summed = jnp.sum(contracted * factor_c[...].astype(jnp.float32)[None], axis=1)
        for h in range(rank // LANES):
            out[i, pl.ds((SLOTS + h) * GROUP, rows), :] = summed[:, h * LANES : (h + 1) * LANES]
        return carry

    lax.fori_loop(0, PARTS, contract, 0)


def first_solve_kernel(where, gathered, factor_c, a_hat, slab, work, inverse, raw):
    rank = work.shape[0]
    share = rank // PARTS
    bands = [
        jnp.concatenate([gathered[p, t * GROUP : (t + 1) * GROUP, :] for p in range(PARTS)], axis=0)
        for t in range(SLOTS + rank // LANES)
    ]
    b_gram = unpacked_gram(bands[:SLOTS])
    m_first = jnp.concatenate(bands[SLOTS:], axis=1)
    row, _ = invert_scaled(b_gram * bf16_gram(factor_c[...]), work, inverse)
    rows = dot_nn(m_first * row, inverse[...]) * row
    a_hat[...] = rows
    raw[...] = dot_tn(rows, rows)
    mine = raw[pl.ds(where[0] * share, share), :]
    squares = jnp.sum(rows * rows, axis=0, keepdims=True)
    for p in range(PARTS):
        top, left = (p // 2) * GROUP, (p % 2) * LANES
        slab[p, 0:GROUP, :] = mine[top : top + GROUP, left : left + LANES]
        slab[p, GROUP:, :] = jnp.zeros((GROUP, LANES), jnp.float32)
        for h in range(rank // LANES):
            slab[p, GROUP + h : GROUP + h + 1, :] = squares[:, h * LANES : (h + 1) * LANES]


def assemble(pieces):
    bands = []
    for q in range(PARTS):
        for p in range(0, PARTS, 2):
            bands.append(jnp.concatenate([pieces[q, p], pieces[q, p + 1]], axis=1))
    return jnp.concatenate(bands, axis=0)


def norm_row(sums):
    squares = total(sums[p, GROUP:, :] for p in range(PARTS))
    return jnp.sqrt(jnp.concatenate([squares[0:1], squares[1:2]], axis=1) + EPSILON)


def second_mode_kernel(
    tensor_in, a_hat_in, sums_in, factor_c_in, out, tensor, a_hat, sums, factor_c, arrived, arrived_small
):
    x_rows, time_len, depth = tensor.shape
    rank = a_hat.shape[1]
    rows, band = JOINED * x_rows // PARTS, depth // PARTS
    small = fetch_small([sums_in, a_hat_in, factor_c_in], [sums, a_hat, factor_c], arrived_small)
    wait_part = fetch_parts(tensor_in, tensor, arrived)
    for one in small:
        one.wait()
    norms = norm_row(sums)
    tile = total(sums[p, 0:GROUP, :] for p in range(PARTS))
    for p in range(PARTS):
        out[p, band:, 0:LANES] = tile
        out[p, band:, LANES:] = jnp.zeros((GROUP, rank - LANES), jnp.float32)
    out[:, 0:band, :] = jnp.zeros((PARTS, band, rank), jnp.float32)

    def contract(i, carry):
        for n in range(JOINED):
            wait_part(i * JOINED + n)
        a_unit = a_hat[pl.ds(i * rows, rows), :] / norms
        khatri_rao = (a_unit[:, None, :] * factor_c[...].astype(jnp.float32)[None]).astype(jnp.bfloat16)
        out[:, 0:band, :] += lax.dot_general(
            tensor[pl.ds(i * rows, rows)].reshape(rows * time_len, depth),
            khatri_rao.reshape(rows * time_len, rank),
            (((0,), (0,)), ((), ())),
            preferred_element_type=jnp.float32,
        ).reshape(PARTS, band, rank)
        return carry

    lax.fori_loop(0, PARTS // JOINED, contract, 0)


def second_inverse_kernel(pieces, sums, factor_c, inverse, work):
    raw = assemble(pieces)
    norms = norm_row(sums)
    norms_down = jnp.sum(jnp.where(diagonal_mask(raw.shape[0]), norms, 0.0), axis=1, keepdims=True)
    row, col = invert_scaled(raw * bf16_gram(factor_c[...]), work, inverse)
    inverse[...] = inverse[...] * (row * norms) * (col * norms_down)


def second_solve_kernel(m_second, inverse, b_hat):
    b_hat[...] = dot_nn(total(m_second[p] for p in range(PARTS)), inverse[...])


def f32(*shape):
    return jax.ShapeDtypeStruct(shape, jnp.float32)


def call(kernel, out_shape, *operands, scratch=(), vmem=VMEM_BYTES, **more):
    return pl.pallas_call(
        kernel,
        out_shape=out_shape,
        scratch_shapes=list(scratch),
        compiler_params=pltpu.CompilerParams(vmem_limit_bytes=vmem),
        **more,
    )(*operands)


def stream(kernel, out_shape, *operands):
    return call(
        kernel,
        out_shape,
        *operands,
        scratch=[
            *(pltpu.VMEM(x.shape, x.dtype) for x in operands),
            pltpu.SemaphoreType.DMA((PARTS,)),
            pltpu.SemaphoreType.DMA((len(operands) - 1,)),
        ],
        vmem=STREAM_BYTES,
        in_specs=[pl.BlockSpec(memory_space=pl.ANY)] * len(operands),
    )


def scatter_sum(parts, axis):
    return jnp.sum(lax.all_to_all(parts, axis, 0, 0), axis=0)


def gather(block, axis):
    return lax.all_to_all(jnp.broadcast_to(block[None], (PARTS, *block.shape)), axis, 0, 0)


def local(tensor, factor_b, factor_c):
    x_rows, time_len, y_rows = tensor.shape
    rank = factor_b.shape[1]
    square = pltpu.VMEM((rank, rank), jnp.float32)

    whole = pl.BlockSpec(memory_space=pltpu.VMEM)
    first = stream(
        first_mode_kernel, f32(PARTS, (SLOTS + rank // LANES) * GROUP, LANES), tensor, factor_b, factor_c
    )
    gathered = gather(scatter_sum(first, "gy"), "gy")

    where = lax.axis_index("gy").astype(jnp.int32).reshape(1)
    a_hat, slab = call(
        first_solve_kernel,
        (f32(x_rows, rank), f32(PARTS, 2 * GROUP, LANES)),
        where,
        gathered,
        factor_c,
        scratch=[square, square, square],
        in_specs=[pl.BlockSpec(memory_space=pltpu.SMEM), whole, whole],
    )

    sums = gather(scatter_sum(slab, "gl"), "gh")
    product = stream(
        second_mode_kernel, f32(PARTS, y_rows // PARTS + GROUP, rank), tensor, a_hat, sums, factor_c
    )
    received = lax.all_to_all(product, "gl", 0, 0)
    m_second = gather(jnp.sum(received[:, : y_rows // PARTS], axis=0), "gh")
    pieces = lax.all_gather(received[:, y_rows // PARTS :, :LANES], "gy")
    inverse = call(
        second_inverse_kernel, f32(rank, rank), pieces, sums, factor_c, scratch=[square], cost_estimate=INVERSE_COST
    )
    b_band = call(second_solve_kernel, f32(y_rows // PARTS, rank), m_second, inverse)
    b_hat = gather(b_band, "gl").reshape(y_rows, rank)
    return (a_hat, b_hat)


def solution(mesh):
    split = Mesh(mesh.devices.reshape(PARTS, PARTS, PARTS), ("gh", "gl", "gy"))
    x_axes = ("gh", "gl")
    return jax.shard_map(
        local,
        mesh=split,
        in_specs=(P(x_axes, None, "gy"), P("gy", None), P()),
        out_specs=(P(x_axes, None), P("gy", None)),
        check_vma=False,
    )
```

```python
import functools

import jax
import jax.numpy as jnp
from jax import lax
from jax.experimental import pallas as pl
from jax.experimental.pallas import tpu as pltpu
from jax.sharding import Mesh
from jax.sharding import PartitionSpec as P

EPSILON = 1e-06
HIGH = lax.Precision.HIGHEST
BLOCK = 64
GROUP = 8
LANES = 128
JOINED = 2
SLOTS = 5
PARTS = 8
AHEAD = 2
STEPS = 12
RESIDUAL = 1e-8
VMEM_BYTES = 24 * 1024 * 1024
STREAM_BYTES = 115 * 512 * 1024
INVERSE_COST = pl.CostEstimate(flops=12_000_000_000, bytes_accessed=1_000_000, transcendentals=0)


def dot_nn(left, right):
    return lax.dot_general(left, right, (((1,), (0,)), ((), ())), precision=HIGH, preferred_element_type=jnp.float32)


def dot_tn(left, right):
    return lax.dot_general(left, right, (((0,), (0,)), ((), ())), precision=HIGH, preferred_element_type=jnp.float32)


def bf16_gram(factor):
    return lax.dot_general(factor, factor, (((0,), (0,)), ((), ())), preferred_element_type=jnp.float32)


def total(terms):
    terms = list(terms)
    while len(terms) > 1:
        paired = [terms[i] + terms[i + 1] for i in range(0, len(terms) - 1, 2)]
        terms = paired + ([terms[-1]] if len(terms) % 2 else [])
    return terms[0]


def solve_group(entries, rows):
    n = len(rows)
    e = [list(line) for line in entries]
    rows = list(rows)
    factors, scaled = {}, [None] * n
    for p in range(0, n, 2):
        a, b, c = e[p][p], e[p][p + 1], e[p + 1][p + 1]
        inv_det = pltpu.reciprocal(a * c - b * b, approx=True)
        inv_a, inv_b, inv_c = c * inv_det, b * inv_det, a * inv_det
        for i in range(p + 2, n):
            x, y = e[p][i], e[p + 1][i]
            f0, f1 = inv_a * x - inv_b * y, inv_c * y - inv_b * x
            factors[p, i] = f0, f1
            for j in range(i, n):
                e[i][j] = e[i][j] - (f0 * e[p][j] + f1 * e[p + 1][j])
            rows[i] = rows[i] - (f0 * rows[p] + f1 * rows[p + 1])
        scaled[p] = inv_a * rows[p] - inv_b * rows[p + 1]
        scaled[p + 1] = inv_c * rows[p + 1] - inv_b * rows[p]
    for p in range(n - 4, -1, -2):
        for q in range(2):
            scaled[p + q] = scaled[p + q] - total(factors[p, i][q] * scaled[i] for i in range(p + 2, n))
    return scaled


def block_inverse(block):
    order = block.shape[0]
    width = 2 * order
    count = order // GROUP
    eye = (
        lax.broadcasted_iota(jnp.int32, (order, order), 0) == lax.broadcasted_iota(jnp.int32, (order, order), 1)
    ).astype(jnp.float32)
    wide = jnp.concatenate([block, eye], axis=1)
    groups = [wide[g * GROUP : (g + 1) * GROUP] for g in range(count)]
    sub = lax.broadcasted_iota(jnp.int32, (GROUP, width), 0)
    full = (GROUP, width)
    for g in range(count):
        k = g * GROUP
        rows = [jnp.broadcast_to(groups[g][i : i + 1], full) for i in range(GROUP)]
        entries = [
            [jnp.broadcast_to(rows[i][:, k + j : k + j + 1], full) if j >= i else None for j in range(GROUP)]
            for i in range(GROUP)
        ]
        steps = solve_group(entries, rows)
        order_of = [h for h in range(g + 1, count)] + [h for h in range(g)]
        for h in order_of:
            cols = [jnp.broadcast_to(groups[h][:, k + j : k + j + 1], full) for j in range(GROUP)]
            groups[h] = groups[h] - total(cols[j] * steps[j] for j in range(GROUP))
        packed = steps[0]
        for i in range(1, GROUP):
            packed = jnp.where(sub == i, steps[i], packed)
        groups[g] = packed
    return jnp.concatenate([x[:, order:] for x in groups], axis=0)


def invert(work):
    order = work.shape[0]

    def sweep(_, carry):
        head = work[0:BLOCK, :]
        inv = block_inverse(head[:, 0:BLOCK])
        lane = lax.broadcasted_iota(jnp.int32, (BLOCK, order), 1)
        row = lax.broadcasted_iota(jnp.int32, (BLOCK, order), 0)
        band = dot_nn(inv, jnp.where(lane < BLOCK, (lane == row).astype(jnp.float32), head))
        rest = work[BLOCK:order, :]
        lane_low = lax.broadcasted_iota(jnp.int32, (order - BLOCK, order), 1)
        lower = jnp.where(lane_low < BLOCK, 0.0, rest) - dot_nn(rest[:, 0:BLOCK], band)
        work[0 : order - BLOCK, :] = pltpu.roll(lower, order - BLOCK, 1)
        work[order - BLOCK : order, :] = pltpu.roll(band, order - BLOCK, 1)
        return carry

    lax.fori_loop(0, order // BLOCK, sweep, 0)


def diagonal_mask(order):
    return lax.broadcasted_iota(jnp.int32, (order, order), 0) == lax.broadcasted_iota(jnp.int32, (order, order), 1)


def invert_scaled(matrix, work, inverse):
    order = matrix.shape[0]
    diagonal = diagonal_mask(order)
    kept = jnp.where(diagonal, matrix, 0.0)
    row = 1.0 / jnp.sqrt(jnp.sum(kept, axis=0, keepdims=True))
    col = 1.0 / jnp.sqrt(jnp.sum(kept, axis=1, keepdims=True))
    scaled = jnp.where(diagonal, 1.0, matrix * row * col)
    work[...] = scaled
    bound = jnp.max(jnp.sum(jnp.abs(scaled), axis=0, keepdims=True))
    size = jnp.where(bound < 2.0, 1.0, 1.0 / bound)
    inverse[...] = jnp.where(diagonal, 2.0 * size, 0.0) - (size * size) * scaled

    def unfinished(carry):
        residual, step = carry
        return (residual > RESIDUAL) & (step < STEPS)

    def improve(carry):
        step = carry[1]
        guess = inverse[...]
        error = jnp.where(diagonal_mask(order), 1.0, 0.0) - dot_nn(work[...], guess)
        inverse[...] = guess + dot_nn(guess, error)
        return jnp.sum(error * error), step + 1

    carry = (jnp.float32(1.0), jnp.int32(0))
    for _ in range(2):
        carry = improve(carry)
    residual, _ = lax.while_loop(unfinished, improve, carry)

    @pl.when(jnp.logical_not(residual <= RESIDUAL))
    def _():
        invert(work)
        inverse[...] = work[...]

    return row, col


def fetch(tensor_in, tensor, small_in, small, arrived, arrived_small):
    rows = tensor.shape[0] // PARTS

    def copy(i):
        part = pl.ds(i * rows, rows)
        return pltpu.make_async_copy(tensor_in.at[part], tensor.at[part], arrived.at[i])

    copies = [pltpu.make_async_copy(s, t, arrived_small.at[n]) for n, (s, t) in enumerate(zip(small_in, small))]
    for one in copies:
        one.start()
    for i in range(AHEAD):
        copy(i).start()
    for one in copies:
        one.wait()
    for i in range(AHEAD, PARTS):
        copy(i).start()
    return lambda i: copy(i).wait()


def packed_gram(gram):
    low = lax.broadcasted_iota(jnp.int32, (BLOCK, LANES), 1) < BLOCK
    return [
        gram[0:64, 0:128],
        gram[128:192, 0:128],
        gram[192:256, 0:128],
        gram[192:256, 128:256],
        jnp.where(low, gram[128:192, 128:256], gram[64:128, 0:128]),
    ]


def unpacked_gram(slots):
    low = lax.broadcasted_iota(jnp.int32, (BLOCK, LANES), 1) < BLOCK
    none = jnp.zeros((BLOCK, LANES), jnp.float32)
    half = jnp.concatenate(
        [
            jnp.concatenate([slots[0], none], axis=1),
            jnp.concatenate([jnp.where(low, 0.0, slots[4]), none], axis=1),
            jnp.concatenate([slots[1], jnp.where(low, slots[4], 0.0)], axis=1),
            jnp.concatenate([slots[2], slots[3]], axis=1),
        ],
        axis=0,
    )
    shape = half.shape
    row_block = lax.broadcasted_iota(jnp.int32, shape, 0) // BLOCK
    col_block = lax.broadcasted_iota(jnp.int32, shape, 1) // BLOCK
    return half + jnp.where(row_block == col_block, 0.0, half).T


def first_mode_kernel(tensor_in, factor_b_in, factor_c_in, out, tensor, factor_b, factor_c, arrived, arrived_small):
    x_rows, time_len, depth = tensor.shape
    rank = factor_b.shape[1]
    rows = x_rows // PARTS
    wait_part = fetch(
        tensor_in, tensor, [factor_b_in, factor_c_in], [factor_b, factor_c], arrived, arrived_small
    )
    for t, slot in enumerate(packed_gram(bf16_gram(factor_b[...]))):
        for i in range(PARTS):
            out[i, t * GROUP : (t + 1) * GROUP, :] = slot[i * GROUP : (i + 1) * GROUP]

    def contract(i, carry):
        wait_part(i)
        contracted = jnp.dot(
            tensor[pl.ds(i * rows, rows)].reshape(rows * time_len, depth),
            factor_b[...],
            preferred_element_type=jnp.float32,
        ).reshape(rows, time_len, rank)
        summed = jnp.sum(contracted * factor_c[...].astype(jnp.float32)[None], axis=1)
        for h in range(rank // LANES):
            out[i, pl.ds((SLOTS + h) * GROUP, rows), :] = summed[:, h * LANES : (h + 1) * LANES]
        return carry

    lax.fori_loop(0, PARTS, contract, 0)


def first_solve_kernel(where, gathered, factor_c, a_hat, slab, work, inverse, raw):
    rank = work.shape[0]
    share = rank // PARTS
    bands = [
        jnp.concatenate([gathered[p, t * GROUP : (t + 1) * GROUP, :] for p in range(PARTS)], axis=0)
        for t in range(SLOTS + rank // LANES)
    ]
    b_gram = unpacked_gram(bands[:SLOTS])
    m_first = jnp.concatenate(bands[SLOTS:], axis=1)
    row, _ = invert_scaled(b_gram * bf16_gram(factor_c[...]), work, inverse)
    rows = dot_nn(m_first * row, inverse[...]) * row
    a_hat[...] = rows
    raw[...] = dot_tn(rows, rows)
    mine = raw[pl.ds(where[0] * share, share), :]
    squares = jnp.sum(rows * rows, axis=0, keepdims=True)
    for p in range(PARTS):
        top, left = (p // 2) * GROUP, (p % 2) * LANES
        slab[p, 0:GROUP, :] = mine[top : top + GROUP, left : left + LANES]
        slab[p, GROUP:, :] = jnp.zeros((GROUP, LANES), jnp.float32)
        for h in range(rank // LANES):
            slab[p, GROUP + h : GROUP + h + 1, :] = squares[:, h * LANES : (h + 1) * LANES]


def assemble(pieces):
    bands = []
    for q in range(PARTS):
        for p in range(0, PARTS, 2):
            bands.append(jnp.concatenate([pieces[q, p], pieces[q, p + 1]], axis=1))
    return jnp.concatenate(bands, axis=0)


def norm_row(sums):
    squares = total(sums[p, GROUP:, :] for p in range(PARTS))
    return jnp.sqrt(jnp.concatenate([squares[0:1], squares[1:2]], axis=1) + EPSILON)


def second_mode_kernel(
    tensor_in, a_hat_in, sums_in, factor_c_in, out, tensor, a_hat, sums, factor_c, arrived, arrived_small
):
    x_rows, time_len, depth = tensor.shape
    rank = a_hat.shape[1]
    rows, band = JOINED * x_rows // PARTS, depth // PARTS
    wait_part = fetch(
        tensor_in, tensor, [sums_in, a_hat_in, factor_c_in], [sums, a_hat, factor_c], arrived, arrived_small
    )
    norms = norm_row(sums)
    tile = total(sums[p, 0:GROUP, :] for p in range(PARTS))
    for p in range(PARTS):
        out[p, band:, 0:LANES] = tile
        out[p, band:, LANES:] = jnp.zeros((GROUP, rank - LANES), jnp.float32)
    out[:, 0:band, :] = jnp.zeros((PARTS, band, rank), jnp.float32)

    def contract(i, carry):
        for n in range(JOINED):
            wait_part(i * JOINED + n)
        a_unit = a_hat[pl.ds(i * rows, rows), :] / norms
        khatri_rao = (a_unit[:, None, :] * factor_c[...].astype(jnp.float32)[None]).astype(jnp.bfloat16)
        out[:, 0:band, :] += lax.dot_general(
            tensor[pl.ds(i * rows, rows)].reshape(rows * time_len, depth),
            khatri_rao.reshape(rows * time_len, rank),
            (((0,), (0,)), ((), ())),
            preferred_element_type=jnp.float32,
        ).reshape(PARTS, band, rank)
        return carry

    lax.fori_loop(0, PARTS // JOINED, contract, 0)


def second_inverse_kernel(pieces, sums, factor_c, inverse, work):
    raw = assemble(pieces)
    norms = norm_row(sums)
    norms_down = jnp.sum(jnp.where(diagonal_mask(raw.shape[0]), norms, 0.0), axis=1, keepdims=True)
    row, col = invert_scaled(raw * bf16_gram(factor_c[...]), work, inverse)
    inverse[...] = inverse[...] * (row * norms) * (col * norms_down)


def second_solve_kernel(m_second, inverse, b_hat):
    b_hat[...] = dot_nn(total(m_second[p] for p in range(PARTS)), inverse[...])


def f32(*shape):
    return jax.ShapeDtypeStruct(shape, jnp.float32)


def call(kernel, out_shape, *operands, scratch=(), vmem=VMEM_BYTES, **more):
    return pl.pallas_call(
        kernel,
        out_shape=out_shape,
        scratch_shapes=list(scratch),
        compiler_params=pltpu.CompilerParams(vmem_limit_bytes=vmem),
        **more,
    )(*operands)


def stream(kernel, out_shape, *operands):
    return call(
        kernel,
        out_shape,
        *operands,
        scratch=[
            *(pltpu.VMEM(x.shape, x.dtype) for x in operands),
            pltpu.SemaphoreType.DMA((PARTS,)),
            pltpu.SemaphoreType.DMA((len(operands) - 1,)),
        ],
        vmem=STREAM_BYTES,
        in_specs=[pl.BlockSpec(memory_space=pl.ANY)] * len(operands),
    )


def scatter_sum(parts, axis):
    return jnp.sum(lax.all_to_all(parts, axis, 0, 0), axis=0)


def gather(block, axis):
    return lax.all_to_all(jnp.broadcast_to(block[None], (PARTS, *block.shape)), axis, 0, 0)


def local(tensor, factor_b, factor_c):
    x_rows, time_len, y_rows = tensor.shape
    rank = factor_b.shape[1]
    square = pltpu.VMEM((rank, rank), jnp.float32)

    whole = pl.BlockSpec(memory_space=pltpu.VMEM)
    first = stream(
        first_mode_kernel, f32(PARTS, (SLOTS + rank // LANES) * GROUP, LANES), tensor, factor_b, factor_c
    )
    gathered = gather(scatter_sum(first, "gy"), "gy")

    where = lax.axis_index("gy").astype(jnp.int32).reshape(1)
    a_hat, slab = call(
        first_solve_kernel,
        (f32(x_rows, rank), f32(PARTS, 2 * GROUP, LANES)),
        where,
        gathered,
        factor_c,
        scratch=[square, square, square],
        in_specs=[pl.BlockSpec(memory_space=pltpu.SMEM), whole, whole],
    )

    sums = gather(scatter_sum(slab, "gl"), "gh")
    product = stream(
        second_mode_kernel, f32(PARTS, y_rows // PARTS + GROUP, rank), tensor, a_hat, sums, factor_c
    )
    received = lax.all_to_all(product, "gl", 0, 0)
    m_second = gather(jnp.sum(received[:, : y_rows // PARTS], axis=0), "gh")
    pieces = lax.all_gather(received[:, y_rows // PARTS :, :LANES], "gy")
    inverse = call(
        second_inverse_kernel, f32(rank, rank), pieces, sums, factor_c, scratch=[square], cost_estimate=INVERSE_COST
    )
    b_band = call(second_solve_kernel, f32(y_rows // PARTS, rank), m_second, inverse)
    b_hat = gather(b_band, "gl").reshape(y_rows, rank)
    return (a_hat, b_hat)


def solution(mesh):
    split = Mesh(mesh.devices.reshape(PARTS, PARTS, PARTS), ("gh", "gl", "gy"))
    x_axes = ("gh", "gl")
    return jax.shard_map(
        local,
        mesh=split,
        in_specs=(P(x_axes, None, "gy"), P("gy", None), P()),
        out_specs=(P(x_axes, None), P("gy", None)),
        check_vma=False,
    )
```

```python
import functools

import jax
import jax.numpy as jnp
from jax import lax
from jax.experimental import pallas as pl
from jax.experimental.pallas import tpu as pltpu
from jax.sharding import Mesh
from jax.sharding import PartitionSpec as P

EPSILON = 1e-06
HIGH = lax.Precision.HIGHEST
BLOCK = 64
GROUP = 8
LANES = 128
JOINED = 2
SLOTS = 5
PARTS = 8
HALVES = 2
FAR = ("zh", "zb")
AHEAD = 2
STEPS = 12
RESIDUAL = 1e-8
VMEM_BYTES = 24 * 1024 * 1024
STREAM_BYTES = 115 * 512 * 1024
INVERSE_COST = pl.CostEstimate(flops=12_000_000_000, bytes_accessed=1_000_000, transcendentals=0)


def dot_nn(left, right):
    return lax.dot_general(left, right, (((1,), (0,)), ((), ())), precision=HIGH, preferred_element_type=jnp.float32)


def dot_tn(left, right):
    return lax.dot_general(left, right, (((0,), (0,)), ((), ())), precision=HIGH, preferred_element_type=jnp.float32)


def bf16_gram(factor):
    return lax.dot_general(factor, factor, (((0,), (0,)), ((), ())), preferred_element_type=jnp.float32)


def total(terms):
    terms = list(terms)
    while len(terms) > 1:
        paired = [terms[i] + terms[i + 1] for i in range(0, len(terms) - 1, 2)]
        terms = paired + ([terms[-1]] if len(terms) % 2 else [])
    return terms[0]


def solve_group(entries, rows):
    n = len(rows)
    e = [list(line) for line in entries]
    rows = list(rows)
    factors, scaled = {}, [None] * n
    for p in range(0, n, 2):
        a, b, c = e[p][p], e[p][p + 1], e[p + 1][p + 1]
        inv_det = pltpu.reciprocal(a * c - b * b, approx=True)
        inv_a, inv_b, inv_c = c * inv_det, b * inv_det, a * inv_det
        for i in range(p + 2, n):
            x, y = e[p][i], e[p + 1][i]
            f0, f1 = inv_a * x - inv_b * y, inv_c * y - inv_b * x
            factors[p, i] = f0, f1
            for j in range(i, n):
                e[i][j] = e[i][j] - (f0 * e[p][j] + f1 * e[p + 1][j])
            rows[i] = rows[i] - (f0 * rows[p] + f1 * rows[p + 1])
        scaled[p] = inv_a * rows[p] - inv_b * rows[p + 1]
        scaled[p + 1] = inv_c * rows[p + 1] - inv_b * rows[p]
    for p in range(n - 4, -1, -2):
        for q in range(2):
            scaled[p + q] = scaled[p + q] - total(factors[p, i][q] * scaled[i] for i in range(p + 2, n))
    return scaled


def block_inverse(block):
    order = block.shape[0]
    width = 2 * order
    count = order // GROUP
    eye = (
        lax.broadcasted_iota(jnp.int32, (order, order), 0) == lax.broadcasted_iota(jnp.int32, (order, order), 1)
    ).astype(jnp.float32)
    wide = jnp.concatenate([block, eye], axis=1)
    groups = [wide[g * GROUP : (g + 1) * GROUP] for g in range(count)]
    sub = lax.broadcasted_iota(jnp.int32, (GROUP, width), 0)
    full = (GROUP, width)
    for g in range(count):
        k = g * GROUP
        rows = [jnp.broadcast_to(groups[g][i : i + 1], full) for i in range(GROUP)]
        entries = [
            [jnp.broadcast_to(rows[i][:, k + j : k + j + 1], full) if j >= i else None for j in range(GROUP)]
            for i in range(GROUP)
        ]
        steps = solve_group(entries, rows)
        order_of = [h for h in range(g + 1, count)] + [h for h in range(g)]
        for h in order_of:
            cols = [jnp.broadcast_to(groups[h][:, k + j : k + j + 1], full) for j in range(GROUP)]
            groups[h] = groups[h] - total(cols[j] * steps[j] for j in range(GROUP))
        packed = steps[0]
        for i in range(1, GROUP):
            packed = jnp.where(sub == i, steps[i], packed)
        groups[g] = packed
    return jnp.concatenate([x[:, order:] for x in groups], axis=0)


def invert(work):
    order = work.shape[0]

    def sweep(_, carry):
        head = work[0:BLOCK, :]
        inv = block_inverse(head[:, 0:BLOCK])
        lane = lax.broadcasted_iota(jnp.int32, (BLOCK, order), 1)
        row = lax.broadcasted_iota(jnp.int32, (BLOCK, order), 0)
        band = dot_nn(inv, jnp.where(lane < BLOCK, (lane == row).astype(jnp.float32), head))
        rest = work[BLOCK:order, :]
        lane_low = lax.broadcasted_iota(jnp.int32, (order - BLOCK, order), 1)
        lower = jnp.where(lane_low < BLOCK, 0.0, rest) - dot_nn(rest[:, 0:BLOCK], band)
        work[0 : order - BLOCK, :] = pltpu.roll(lower, order - BLOCK, 1)
        work[order - BLOCK : order, :] = pltpu.roll(band, order - BLOCK, 1)
        return carry

    lax.fori_loop(0, order // BLOCK, sweep, 0)


def diagonal_mask(order):
    return lax.broadcasted_iota(jnp.int32, (order, order), 0) == lax.broadcasted_iota(jnp.int32, (order, order), 1)


def invert_scaled(matrix, work, inverse):
    order = matrix.shape[0]
    diagonal = diagonal_mask(order)
    kept = jnp.where(diagonal, matrix, 0.0)
    row = 1.0 / jnp.sqrt(jnp.sum(kept, axis=0, keepdims=True))
    col = 1.0 / jnp.sqrt(jnp.sum(kept, axis=1, keepdims=True))
    scaled = jnp.where(diagonal, 1.0, matrix * row * col)
    work[...] = scaled
    bound = jnp.max(jnp.sum(jnp.abs(scaled), axis=0, keepdims=True))
    size = jnp.where(bound < 2.0, 1.0, 1.0 / bound)
    inverse[...] = jnp.where(diagonal, 2.0 * size, 0.0) - (size * size) * scaled

    def unfinished(carry):
        residual, step = carry
        return (residual > RESIDUAL) & (step < STEPS)

    def improve(carry):
        step = carry[1]
        guess = inverse[...]
        error = jnp.where(diagonal_mask(order), 1.0, 0.0) - dot_nn(work[...], guess)
        inverse[...] = guess + dot_nn(guess, error)
        return jnp.sum(error * error), step + 1

    carry = (jnp.float32(1.0), jnp.int32(0))
    for _ in range(2):
        carry = improve(carry)
    residual, _ = lax.while_loop(unfinished, improve, carry)

    @pl.when(jnp.logical_not(residual <= RESIDUAL))
    def _():
        invert(work)
        inverse[...] = work[...]

    return row, col


def fetch(tensor_in, tensor, small_in, small, arrived, arrived_small):
    rows = tensor.shape[0] // PARTS

    def copy(i):
        part = pl.ds(i * rows, rows)
        return pltpu.make_async_copy(tensor_in.at[part], tensor.at[part], arrived.at[i])

    copies = [pltpu.make_async_copy(s, t, arrived_small.at[n]) for n, (s, t) in enumerate(zip(small_in, small))]
    for one in copies:
        one.start()
    for i in range(AHEAD):
        copy(i).start()
    for one in copies:
        one.wait()
    for i in range(AHEAD, PARTS):
        copy(i).start()
    return lambda i: copy(i).wait()


def packed_gram(gram):
    low = lax.broadcasted_iota(jnp.int32, (BLOCK, LANES), 1) < BLOCK
    return [
        gram[0:64, 0:128],
        gram[128:192, 0:128],
        gram[192:256, 0:128],
        gram[192:256, 128:256],
        jnp.where(low, gram[128:192, 128:256], gram[64:128, 0:128]),
    ]


def unpacked_gram(slots):
    low = lax.broadcasted_iota(jnp.int32, (BLOCK, LANES), 1) < BLOCK
    none = jnp.zeros((BLOCK, LANES), jnp.float32)
    half = jnp.concatenate(
        [
            jnp.concatenate([slots[0], none], axis=1),
            jnp.concatenate([jnp.where(low, 0.0, slots[4]), none], axis=1),
            jnp.concatenate([slots[1], jnp.where(low, slots[4], 0.0)], axis=1),
            jnp.concatenate([slots[2], slots[3]], axis=1),
        ],
        axis=0,
    )
    shape = half.shape
    row_block = lax.broadcasted_iota(jnp.int32, shape, 0) // BLOCK
    col_block = lax.broadcasted_iota(jnp.int32, shape, 1) // BLOCK
    return half + jnp.where(row_block == col_block, 0.0, half).T


def first_mode_kernel(tensor_in, factor_b_in, factor_c_in, out, tensor, factor_b, factor_c, arrived, arrived_small):
    x_rows, time_len, depth = tensor.shape
    rank = factor_b.shape[1]
    rows = x_rows // PARTS
    wait_part = fetch(
        tensor_in, tensor, [factor_b_in, factor_c_in], [factor_b, factor_c], arrived, arrived_small
    )
    for t, slot in enumerate(packed_gram(bf16_gram(factor_b[...]))):
        for i in range(PARTS):
            out[i, t * GROUP : (t + 1) * GROUP, :] = slot[i * GROUP : (i + 1) * GROUP]

    def contract(i, carry):
        wait_part(i)
        contracted = jnp.dot(
            tensor[pl.ds(i * rows, rows)].reshape(rows * time_len, depth),
            factor_b[...],
            preferred_element_type=jnp.float32,
        ).reshape(rows, time_len, rank)
        summed = jnp.sum(contracted * factor_c[...].astype(jnp.float32)[None], axis=1)
        for h in range(rank // LANES):
            out[i, pl.ds((SLOTS + h) * GROUP, rows), :] = summed[:, h * LANES : (h + 1) * LANES]
        return carry

    lax.fori_loop(0, PARTS, contract, 0)


def first_solve_kernel(where, gathered, factor_c, a_hat, slab, work, inverse, raw):
    rank = work.shape[0]
    share = rank // PARTS
    bands = [
        jnp.concatenate([gathered[p, t * GROUP : (t + 1) * GROUP, :] for p in range(PARTS)], axis=0)
        for t in range(SLOTS + rank // LANES)
    ]
    b_gram = unpacked_gram(bands[:SLOTS])
    m_first = jnp.concatenate(bands[SLOTS:], axis=1)
    row, _ = invert_scaled(b_gram * bf16_gram(factor_c[...]), work, inverse)
    rows = dot_nn(m_first * row, inverse[...]) * row
    a_hat[...] = rows
    raw[...] = dot_tn(rows, rows)
    mine = raw[pl.ds(where[0] * share, share), :]
    squares = jnp.sum(rows * rows, axis=0, keepdims=True)
    for p in range(PARTS):
        top, left = (p // 2) * GROUP, (p % 2) * LANES
        slab[p, 0:GROUP, :] = mine[top : top + GROUP, left : left + LANES]
        slab[p, GROUP:, :] = jnp.zeros((GROUP, LANES), jnp.float32)
        for h in range(rank // LANES):
            slab[p, GROUP + h : GROUP + h + 1, :] = squares[:, h * LANES : (h + 1) * LANES]


def assemble(pieces):
    bands = []
    for q in range(PARTS):
        for p in range(0, PARTS, 2):
            bands.append(jnp.concatenate([pieces[q, p], pieces[q, p + 1]], axis=1))
    return jnp.concatenate(bands, axis=0)


def norm_row(sums):
    squares = total(sums[p, GROUP:, :] for p in range(PARTS))
    return jnp.sqrt(jnp.concatenate([squares[0:1], squares[1:2]], axis=1) + EPSILON)


def second_mode_kernel(
    tensor_in, a_hat_in, sums_in, factor_c_in, out, tensor, a_hat, sums, factor_c, arrived, arrived_small
):
    x_rows, time_len, depth = tensor.shape
    rank = a_hat.shape[1]
    rows, band = JOINED * x_rows // PARTS, depth // PARTS
    wait_part = fetch(
        tensor_in, tensor, [sums_in, a_hat_in, factor_c_in], [sums, a_hat, factor_c], arrived, arrived_small
    )
    norms = norm_row(sums)
    tile = total(sums[p, 0:GROUP, :] for p in range(PARTS))
    for p in range(PARTS):
        out[p, band:, 0:LANES] = tile
        out[p, band:, LANES:] = jnp.zeros((GROUP, rank - LANES), jnp.float32)
    out[:, 0:band, :] = jnp.zeros((PARTS, band, rank), jnp.float32)

    def contract(i, carry):
        for n in range(JOINED):
            wait_part(i * JOINED + n)
        a_unit = a_hat[pl.ds(i * rows, rows), :] / norms
        khatri_rao = (a_unit[:, None, :] * factor_c[...].astype(jnp.float32)[None]).astype(jnp.bfloat16)
        out[:, 0:band, :] += lax.dot_general(
            tensor[pl.ds(i * rows, rows)].reshape(rows * time_len, depth),
            khatri_rao.reshape(rows * time_len, rank),
            (((0,), (0,)), ((), ())),
            preferred_element_type=jnp.float32,
        ).reshape(PARTS, band, rank)
        return carry

    lax.fori_loop(0, PARTS // JOINED, contract, 0)


def second_inverse_kernel(pieces, sums, factor_c, inverse, work):
    raw = assemble(pieces)
    norms = norm_row(sums)
    norms_down = jnp.sum(jnp.where(diagonal_mask(raw.shape[0]), norms, 0.0), axis=1, keepdims=True)
    row, col = invert_scaled(raw * bf16_gram(factor_c[...]), work, inverse)
    inverse[...] = inverse[...] * (row * norms) * (col * norms_down)


def second_solve_kernel(m_second, inverse, b_hat):
    b_hat[...] = dot_nn(total(m_second[p] for p in range(PARTS)), inverse[...])


def f32(*shape):
    return jax.ShapeDtypeStruct(shape, jnp.float32)


def call(kernel, out_shape, *operands, scratch=(), vmem=VMEM_BYTES, **more):
    return pl.pallas_call(
        kernel,
        out_shape=out_shape,
        scratch_shapes=list(scratch),
        compiler_params=pltpu.CompilerParams(vmem_limit_bytes=vmem),
        **more,
    )(*operands)


def stream(kernel, out_shape, *operands):
    return call(
        kernel,
        out_shape,
        *operands,
        scratch=[
            *(pltpu.VMEM(x.shape, x.dtype) for x in operands),
            pltpu.SemaphoreType.DMA((PARTS,)),
            pltpu.SemaphoreType.DMA((len(operands) - 1,)),
        ],
        vmem=STREAM_BYTES,
        in_specs=[pl.BlockSpec(memory_space=pl.ANY)] * len(operands),
    )


def scatter_sum(parts, axis):
    return jnp.sum(lax.all_to_all(parts, axis, 0, 0), axis=0)


def gather(block, axis, size=PARTS):
    return lax.all_to_all(jnp.broadcast_to(block[None], (size, *block.shape)), axis, 0, 0)


def local(tensor, factor_b, factor_c):
    x_rows, time_len, y_rows = tensor.shape
    rank = factor_b.shape[1]
    square = pltpu.VMEM((rank, rank), jnp.float32)

    whole = pl.BlockSpec(memory_space=pltpu.VMEM)
    first = stream(
        first_mode_kernel, f32(PARTS, (SLOTS + rank // LANES) * GROUP, LANES), tensor, factor_b, factor_c
    )
    gathered = gather(scatter_sum(first, "gy"), "gy")

    where = lax.axis_index("gy").astype(jnp.int32).reshape(1)
    a_hat, slab = call(
        first_solve_kernel,
        (f32(x_rows, rank), f32(PARTS, 2 * GROUP, LANES)),
        where,
        gathered,
        factor_c,
        scratch=[square, square, square],
        in_specs=[pl.BlockSpec(memory_space=pltpu.SMEM), whole, whole],
    )

    sums = gather(scatter_sum(slab, "gl"), FAR)
    product = stream(
        second_mode_kernel, f32(PARTS, y_rows // PARTS + GROUP, rank), tensor, a_hat, sums, factor_c
    )
    received = lax.all_to_all(product, "gl", 0, 0)
    halves = jnp.sum(received[:, : y_rows // PARTS], axis=0).reshape(HALVES, y_rows // PARTS // HALVES, rank)
    repeated = jnp.broadcast_to(halves[None], (PARTS // HALVES, *halves.shape)).reshape(PARTS, *halves.shape[1:])
    m_second = lax.all_to_all(repeated, FAR, 0, 0)
    pieces = lax.all_gather(received[:, y_rows // PARTS :, :LANES], "gy")
    inverse = call(
        second_inverse_kernel, f32(rank, rank), pieces, sums, factor_c, scratch=[square], cost_estimate=INVERSE_COST
    )
    b_band = call(second_solve_kernel, f32(*halves.shape[1:]), m_second, inverse)
    b_hat = gather(b_band, ("gl", "zb"), PARTS * HALVES).reshape(y_rows, rank)
    return (a_hat, b_hat)


def solution(mesh):
    split = Mesh(mesh.devices.reshape(PARTS // HALVES, HALVES, PARTS, PARTS), ("zh", "zb", "gl", "gy"))
    x_axes = (*FAR, "gl")
    return jax.shard_map(
        local,
        mesh=split,
        in_specs=(P(x_axes, None, "gy"), P("gy", None), P()),
        out_specs=(P(x_axes, None), P("gy", None)),
        check_vma=False,
    )
```

```python
import functools

import jax
import jax.numpy as jnp
from jax import lax
from jax.experimental import pallas as pl
from jax.experimental.pallas import tpu as pltpu
from jax.sharding import Mesh
from jax.sharding import PartitionSpec as P

EPSILON = 1e-06
HIGH = lax.Precision.HIGHEST
BLOCK = 64
GROUP = 8
LANES = 128
JOINED = 2
SLOTS = 5
PARTS = 8
HALVES = 2
GY = ("x", "core")
CORES = 2
FAR = ("zh", "zb")
AHEAD = 2
STEPS = 12
RESIDUAL = 1e-8
VMEM_BYTES = 24 * 1024 * 1024
STREAM_BYTES = 115 * 512 * 1024
INVERSE_COST = pl.CostEstimate(flops=12_000_000_000, bytes_accessed=1_000_000, transcendentals=0)


def dot_nn(left, right):
    return lax.dot_general(left, right, (((1,), (0,)), ((), ())), precision=HIGH, preferred_element_type=jnp.float32)


def dot_tn(left, right):
    return lax.dot_general(left, right, (((0,), (0,)), ((), ())), precision=HIGH, preferred_element_type=jnp.float32)


def bf16_gram(factor):
    return lax.dot_general(factor, factor, (((0,), (0,)), ((), ())), preferred_element_type=jnp.float32)


def total(terms):
    terms = list(terms)
    while len(terms) > 1:
        paired = [terms[i] + terms[i + 1] for i in range(0, len(terms) - 1, 2)]
        terms = paired + ([terms[-1]] if len(terms) % 2 else [])
    return terms[0]


def solve_group(entries, rows):
    n = len(rows)
    e = [list(line) for line in entries]
    rows = list(rows)
    factors, scaled = {}, [None] * n
    for p in range(0, n, 2):
        a, b, c = e[p][p], e[p][p + 1], e[p + 1][p + 1]
        inv_det = pltpu.reciprocal(a * c - b * b, approx=True)
        inv_a, inv_b, inv_c = c * inv_det, b * inv_det, a * inv_det
        for i in range(p + 2, n):
            x, y = e[p][i], e[p + 1][i]
            f0, f1 = inv_a * x - inv_b * y, inv_c * y - inv_b * x
            factors[p, i] = f0, f1
            for j in range(i, n):
                e[i][j] = e[i][j] - (f0 * e[p][j] + f1 * e[p + 1][j])
            rows[i] = rows[i] - (f0 * rows[p] + f1 * rows[p + 1])
        scaled[p] = inv_a * rows[p] - inv_b * rows[p + 1]
        scaled[p + 1] = inv_c * rows[p + 1] - inv_b * rows[p]
    for p in range(n - 4, -1, -2):
        for q in range(2):
            scaled[p + q] = scaled[p + q] - total(factors[p, i][q] * scaled[i] for i in range(p + 2, n))
    return scaled


def block_inverse(block):
    order = block.shape[0]
    width = 2 * order
    count = order // GROUP
    eye = (
        lax.broadcasted_iota(jnp.int32, (order, order), 0) == lax.broadcasted_iota(jnp.int32, (order, order), 1)
    ).astype(jnp.float32)
    wide = jnp.concatenate([block, eye], axis=1)
    groups = [wide[g * GROUP : (g + 1) * GROUP] for g in range(count)]
    sub = lax.broadcasted_iota(jnp.int32, (GROUP, width), 0)
    full = (GROUP, width)
    for g in range(count):
        k = g * GROUP
        rows = [jnp.broadcast_to(groups[g][i : i + 1], full) for i in range(GROUP)]
        entries = [
            [jnp.broadcast_to(rows[i][:, k + j : k + j + 1], full) if j >= i else None for j in range(GROUP)]
            for i in range(GROUP)
        ]
        steps = solve_group(entries, rows)
        order_of = [h for h in range(g + 1, count)] + [h for h in range(g)]
        for h in order_of:
            cols = [jnp.broadcast_to(groups[h][:, k + j : k + j + 1], full) for j in range(GROUP)]
            groups[h] = groups[h] - total(cols[j] * steps[j] for j in range(GROUP))
        packed = steps[0]
        for i in range(1, GROUP):
            packed = jnp.where(sub == i, steps[i], packed)
        groups[g] = packed
    return jnp.concatenate([x[:, order:] for x in groups], axis=0)


def invert(work):
    order = work.shape[0]

    def sweep(_, carry):
        head = work[0:BLOCK, :]
        inv = block_inverse(head[:, 0:BLOCK])
        lane = lax.broadcasted_iota(jnp.int32, (BLOCK, order), 1)
        row = lax.broadcasted_iota(jnp.int32, (BLOCK, order), 0)
        band = dot_nn(inv, jnp.where(lane < BLOCK, (lane == row).astype(jnp.float32), head))
        rest = work[BLOCK:order, :]
        lane_low = lax.broadcasted_iota(jnp.int32, (order - BLOCK, order), 1)
        lower = jnp.where(lane_low < BLOCK, 0.0, rest) - dot_nn(rest[:, 0:BLOCK], band)
        work[0 : order - BLOCK, :] = pltpu.roll(lower, order - BLOCK, 1)
        work[order - BLOCK : order, :] = pltpu.roll(band, order - BLOCK, 1)
        return carry

    lax.fori_loop(0, order // BLOCK, sweep, 0)


def diagonal_mask(order):
    return lax.broadcasted_iota(jnp.int32, (order, order), 0) == lax.broadcasted_iota(jnp.int32, (order, order), 1)


def invert_scaled(matrix, work, inverse):
    order = matrix.shape[0]
    diagonal = diagonal_mask(order)
    kept = jnp.where(diagonal, matrix, 0.0)
    row = 1.0 / jnp.sqrt(jnp.sum(kept, axis=0, keepdims=True))
    col = 1.0 / jnp.sqrt(jnp.sum(kept, axis=1, keepdims=True))
    scaled = jnp.where(diagonal, 1.0, matrix * row * col)
    work[...] = scaled
    bound = jnp.max(jnp.sum(jnp.abs(scaled), axis=0, keepdims=True))
    size = jnp.where(bound < 2.0, 1.0, 1.0 / bound)
    inverse[...] = jnp.where(diagonal, 2.0 * size, 0.0) - (size * size) * scaled

    def unfinished(carry):
        residual, step = carry
        return (residual > RESIDUAL) & (step < STEPS)

    def improve(carry):
        step = carry[1]
        guess = inverse[...]
        error = jnp.where(diagonal_mask(order), 1.0, 0.0) - dot_nn(work[...], guess)
        inverse[...] = guess + dot_nn(guess, error)
        return jnp.sum(error * error), step + 1

    carry = (jnp.float32(1.0), jnp.int32(0))
    for _ in range(2):
        carry = improve(carry)
    residual, _ = lax.while_loop(unfinished, improve, carry)

    @pl.when(jnp.logical_not(residual <= RESIDUAL))
    def _():
        invert(work)
        inverse[...] = work[...]

    return row, col


def fetch(tensor_in, tensor, small_in, small, arrived, arrived_small):
    rows = tensor.shape[0] // PARTS

    def copy(i):
        part = pl.ds(i * rows, rows)
        return pltpu.make_async_copy(tensor_in.at[part], tensor.at[part], arrived.at[i])

    copies = [pltpu.make_async_copy(s, t, arrived_small.at[n]) for n, (s, t) in enumerate(zip(small_in, small))]
    for one in copies:
        one.start()
    for i in range(AHEAD):
        copy(i).start()
    for one in copies:
        one.wait()
    for i in range(AHEAD, PARTS):
        copy(i).start()
    return lambda i: copy(i).wait()


def packed_gram(gram):
    low = lax.broadcasted_iota(jnp.int32, (BLOCK, LANES), 1) < BLOCK
    return [
        gram[0:64, 0:128],
        gram[128:192, 0:128],
        gram[192:256, 0:128],
        gram[192:256, 128:256],
        jnp.where(low, gram[128:192, 128:256], gram[64:128, 0:128]),
    ]


def unpacked_gram(slots):
    low = lax.broadcasted_iota(jnp.int32, (BLOCK, LANES), 1) < BLOCK
    none = jnp.zeros((BLOCK, LANES), jnp.float32)
    half = jnp.concatenate(
        [
            jnp.concatenate([slots[0], none], axis=1),
            jnp.concatenate([jnp.where(low, 0.0, slots[4]), none], axis=1),
            jnp.concatenate([slots[1], jnp.where(low, slots[4], 0.0)], axis=1),
            jnp.concatenate([slots[2], slots[3]], axis=1),
        ],
        axis=0,
    )
    shape = half.shape
    row_block = lax.broadcasted_iota(jnp.int32, shape, 0) // BLOCK
    col_block = lax.broadcasted_iota(jnp.int32, shape, 1) // BLOCK
    return half + jnp.where(row_block == col_block, 0.0, half).T


def first_mode_kernel(
    core, tensor_in, factor_b_in, factor_c_in, out, tensor, factor_b, factor_c, arrived, arrived_small
):
    x_rows, time_len, depth = tensor.shape
    rank = factor_b.shape[1]
    rows = x_rows // PARTS
    wait_part = fetch(
        tensor_in, tensor, [factor_b_in, factor_c_in], [factor_b, factor_c], arrived, arrived_small
    )
    half = PARTS // CORES
    for t, slot in enumerate(packed_gram(bf16_gram(factor_b[...]))):
        for i in range(PARTS):
            side = core[0] if i < half else 1 - core[0]
            out[side, i % half, t * GROUP : (t + 1) * GROUP, :] = slot[i * GROUP : (i + 1) * GROUP]

    def contract(i, carry):
        wait_part(i)
        contracted = jnp.dot(
            tensor[pl.ds(i * rows, rows)].reshape(rows * time_len, depth),
            factor_b[...],
            preferred_element_type=jnp.float32,
        ).reshape(rows, time_len, rank)
        summed = jnp.sum(contracted * factor_c[...].astype(jnp.float32)[None], axis=1)
        for h in range(rank // LANES):
            side, place = jnp.where(i < half, core[0], 1 - core[0]), jnp.where(i < half, i, i - half)
            out[side, place, pl.ds((SLOTS + h) * GROUP, rows), :] = summed[:, h * LANES : (h + 1) * LANES]
        return carry

    lax.fori_loop(0, PARTS, contract, 0)


def first_solve_kernel(where, mine, other, factor_c, a_hat, slab, work, inverse, raw):
    rank = work.shape[0]
    share = rank // PARTS
    half = PARTS // CORES
    core = where[0] % CORES
    gathered = [jnp.where(core == p // half, mine[p % half], other[p % half]) for p in range(PARTS)]
    bands = [
        jnp.concatenate([gathered[p][t * GROUP : (t + 1) * GROUP] for p in range(PARTS)], axis=0)
        for t in range(SLOTS + rank // LANES)
    ]
    b_gram = unpacked_gram(bands[:SLOTS])
    m_first = jnp.concatenate(bands[SLOTS:], axis=1)
    row, _ = invert_scaled(b_gram * bf16_gram(factor_c[...]), work, inverse)
    rows = dot_nn(m_first * row, inverse[...]) * row
    a_hat[...] = rows
    raw[...] = dot_tn(rows, rows)
    mine = raw[pl.ds(where[0] * share, share), :]
    squares = jnp.sum(rows * rows, axis=0, keepdims=True)
    for p in range(PARTS):
        top, left = (p // 2) * GROUP, (p % 2) * LANES
        slab[p, 0:GROUP, :] = mine[top : top + GROUP, left : left + LANES]
        slab[p, GROUP:, :] = jnp.zeros((GROUP, LANES), jnp.float32)
        for h in range(rank // LANES):
            slab[p, GROUP + h : GROUP + h + 1, :] = squares[:, h * LANES : (h + 1) * LANES]


def assemble(pieces):
    bands = []
    for q in range(PARTS):
        for p in range(0, PARTS, 2):
            bands.append(jnp.concatenate([pieces[q, p], pieces[q, p + 1]], axis=1))
    return jnp.concatenate(bands, axis=0)


def norm_row(sums):
    squares = total(sums[p, GROUP:, :] for p in range(PARTS))
    return jnp.sqrt(jnp.concatenate([squares[0:1], squares[1:2]], axis=1) + EPSILON)


def second_mode_kernel(
    tensor_in, a_hat_in, sums_in, factor_c_in, out, tensor, a_hat, sums, factor_c, arrived, arrived_small
):
    x_rows, time_len, depth = tensor.shape
    rank = a_hat.shape[1]
    rows, band = JOINED * x_rows // PARTS, depth // PARTS
    wait_part = fetch(
        tensor_in, tensor, [sums_in, a_hat_in, factor_c_in], [sums, a_hat, factor_c], arrived, arrived_small
    )
    norms = norm_row(sums)
    tile = total(sums[p, 0:GROUP, :] for p in range(PARTS))
    for p in range(PARTS):
        out[p, band:, 0:LANES] = tile
        out[p, band:, LANES:] = jnp.zeros((GROUP, rank - LANES), jnp.float32)
    out[:, 0:band, :] = jnp.zeros((PARTS, band, rank), jnp.float32)

    def contract(i, carry):
        for n in range(JOINED):
            wait_part(i * JOINED + n)
        a_unit = a_hat[pl.ds(i * rows, rows), :] / norms
        khatri_rao = (a_unit[:, None, :] * factor_c[...].astype(jnp.float32)[None]).astype(jnp.bfloat16)
        out[:, 0:band, :] += lax.dot_general(
            tensor[pl.ds(i * rows, rows)].reshape(rows * time_len, depth),
            khatri_rao.reshape(rows * time_len, rank),
            (((0,), (0,)), ((), ())),
            preferred_element_type=jnp.float32,
        ).reshape(PARTS, band, rank)
        return carry

    lax.fori_loop(0, PARTS // JOINED, contract, 0)


def second_inverse_kernel(pieces, sums, factor_c, inverse, work):
    raw = assemble(pieces)
    norms = norm_row(sums)
    norms_down = jnp.sum(jnp.where(diagonal_mask(raw.shape[0]), norms, 0.0), axis=1, keepdims=True)
    row, col = invert_scaled(raw * bf16_gram(factor_c[...]), work, inverse)
    inverse[...] = inverse[...] * (row * norms) * (col * norms_down)


def second_solve_kernel(m_second, inverse, b_hat):
    b_hat[...] = dot_nn(total(m_second[p] for p in range(PARTS)), inverse[...])


def f32(*shape):
    return jax.ShapeDtypeStruct(shape, jnp.float32)


def call(kernel, out_shape, *operands, scratch=(), vmem=VMEM_BYTES, **more):
    return pl.pallas_call(
        kernel,
        out_shape=out_shape,
        scratch_shapes=list(scratch),
        compiler_params=pltpu.CompilerParams(vmem_limit_bytes=vmem),
        **more,
    )(*operands)


def stream(kernel, out_shape, *operands, scalars=()):
    return call(
        kernel,
        out_shape,
        *scalars,
        *operands,
        scratch=[
            *(pltpu.VMEM(x.shape, x.dtype) for x in operands),
            pltpu.SemaphoreType.DMA((PARTS,)),
            pltpu.SemaphoreType.DMA((len(operands) - 1,)),
        ],
        vmem=STREAM_BYTES,
        in_specs=[pl.BlockSpec(memory_space=pltpu.SMEM)] * len(scalars)
        + [pl.BlockSpec(memory_space=pl.ANY)] * len(operands),
    )


def swap_cores(value):
    return lax.ppermute(value, "core", [(0, 1), (1, 0)])


def scatter_sum(parts, axis):
    return jnp.sum(lax.all_to_all(parts, axis, 0, 0), axis=0)


def gather(block, axis, size=PARTS):
    return lax.all_to_all(jnp.broadcast_to(block[None], (size, *block.shape)), axis, 0, 0)


def local(tensor, factor_b, factor_c):
    x_rows, time_len, y_rows = tensor.shape
    rank = factor_b.shape[1]
    square = pltpu.VMEM((rank, rank), jnp.float32)

    whole = pl.BlockSpec(memory_space=pltpu.VMEM)
    where = lax.axis_index(GY).astype(jnp.int32).reshape(1)
    core = lax.axis_index("core").astype(jnp.int32).reshape(1)
    first = stream(
        first_mode_kernel,
        f32(CORES, PARTS // CORES, (SLOTS + rank // LANES) * GROUP, LANES),
        tensor,
        factor_b,
        factor_c,
        scalars=[core],
    )
    pair = first[0] + swap_cores(first[1])
    mine = jnp.sum(gather(pair, "x", PARTS // CORES), axis=0)
    other = swap_cores(mine)

    a_hat, slab = call(
        first_solve_kernel,
        (f32(x_rows, rank), f32(PARTS, 2 * GROUP, LANES)),
        where,
        mine,
        other,
        factor_c,
        scratch=[square, square, square],
        in_specs=[pl.BlockSpec(memory_space=pltpu.SMEM), whole, whole, whole],
    )

    sums = gather(scatter_sum(slab, "gl"), FAR)
    product = stream(
        second_mode_kernel, f32(PARTS, y_rows // PARTS + GROUP, rank), tensor, a_hat, sums, factor_c
    )
    received = lax.all_to_all(product, "gl", 0, 0)
    halves = jnp.sum(received[:, : y_rows // PARTS], axis=0).reshape(HALVES, y_rows // PARTS // HALVES, rank)
    repeated = jnp.broadcast_to(halves[None], (PARTS // HALVES, *halves.shape)).reshape(PARTS, *halves.shape[1:])
    m_second = lax.all_to_all(repeated, FAR, 0, 0)
    pieces = lax.all_gather(received[:, y_rows // PARTS :, :LANES], GY)
    inverse = call(
        second_inverse_kernel, f32(rank, rank), pieces, sums, factor_c, scratch=[square], cost_estimate=INVERSE_COST
    )
    b_band = call(second_solve_kernel, f32(*halves.shape[1:]), m_second, inverse)
    b_hat = gather(b_band, ("gl", "zb"), PARTS * HALVES).reshape(y_rows, rank)
    return (a_hat, b_hat)


def solution(mesh):
    z_and_y = (PARTS // HALVES, HALVES, PARTS)
    split = Mesh(mesh.devices.reshape(*z_and_y, PARTS // CORES, CORES), (*FAR, "gl", *GY))
    x_axes = (*FAR, "gl")
    return jax.shard_map(
        local,
        mesh=split,
        in_specs=(P(x_axes, None, GY), P(GY, None), P()),
        out_specs=(P(x_axes, None), P(GY, None)),
        check_vma=False,
    )
```

```python
import functools

import jax
import jax.numpy as jnp
from jax import lax
from jax.experimental import pallas as pl
from jax.experimental.pallas import tpu as pltpu
from jax.sharding import Mesh
from jax.sharding import PartitionSpec as P

EPSILON = 1e-06
HIGH = lax.Precision.HIGHEST
BLOCK = 64
GROUP = 8
LANES = 128
JOINED = 2
SLOTS = 5
PARTS = 8
HALVES = 2
GY = ("x", "core")
CORES = 2
FAR = ("zh", "zb")
AHEAD = 2
STEPS = 12
RESIDUAL = 1e-8
VMEM_BYTES = 24 * 1024 * 1024
STREAM_BYTES = 115 * 512 * 1024
INVERSE_COST = pl.CostEstimate(flops=12_000_000_000, bytes_accessed=1_000_000, transcendentals=0)


def dot_nn(left, right):
    return lax.dot_general(left, right, (((1,), (0,)), ((), ())), precision=HIGH, preferred_element_type=jnp.float32)


def dot_tn(left, right):
    return lax.dot_general(left, right, (((0,), (0,)), ((), ())), precision=HIGH, preferred_element_type=jnp.float32)


def bf16_gram(factor):
    return lax.dot_general(factor, factor, (((0,), (0,)), ((), ())), preferred_element_type=jnp.float32)


def total(terms):
    terms = list(terms)
    while len(terms) > 1:
        paired = [terms[i] + terms[i + 1] for i in range(0, len(terms) - 1, 2)]
        terms = paired + ([terms[-1]] if len(terms) % 2 else [])
    return terms[0]


def solve_group(entries, rows):
    n = len(rows)
    e = [list(line) for line in entries]
    rows = list(rows)
    factors, scaled = {}, [None] * n
    for p in range(0, n, 2):
        a, b, c = e[p][p], e[p][p + 1], e[p + 1][p + 1]
        inv_det = pltpu.reciprocal(a * c - b * b, approx=True)
        inv_a, inv_b, inv_c = c * inv_det, b * inv_det, a * inv_det
        for i in range(p + 2, n):
            x, y = e[p][i], e[p + 1][i]
            f0, f1 = inv_a * x - inv_b * y, inv_c * y - inv_b * x
            factors[p, i] = f0, f1
            for j in range(i, n):
                e[i][j] = e[i][j] - (f0 * e[p][j] + f1 * e[p + 1][j])
            rows[i] = rows[i] - (f0 * rows[p] + f1 * rows[p + 1])
        scaled[p] = inv_a * rows[p] - inv_b * rows[p + 1]
        scaled[p + 1] = inv_c * rows[p + 1] - inv_b * rows[p]
    for p in range(n - 4, -1, -2):
        for q in range(2):
            scaled[p + q] = scaled[p + q] - total(factors[p, i][q] * scaled[i] for i in range(p + 2, n))
    return scaled


def block_inverse(block):
    order = block.shape[0]
    width = 2 * order
    count = order // GROUP
    eye = (
        lax.broadcasted_iota(jnp.int32, (order, order), 0) == lax.broadcasted_iota(jnp.int32, (order, order), 1)
    ).astype(jnp.float32)
    wide = jnp.concatenate([block, eye], axis=1)
    groups = [wide[g * GROUP : (g + 1) * GROUP] for g in range(count)]
    sub = lax.broadcasted_iota(jnp.int32, (GROUP, width), 0)
    full = (GROUP, width)
    for g in range(count):
        k = g * GROUP
        rows = [jnp.broadcast_to(groups[g][i : i + 1], full) for i in range(GROUP)]
        entries = [
            [jnp.broadcast_to(rows[i][:, k + j : k + j + 1], full) if j >= i else None for j in range(GROUP)]
            for i in range(GROUP)
        ]
        steps = solve_group(entries, rows)
        order_of = [h for h in range(g + 1, count)] + [h for h in range(g)]
        for h in order_of:
            cols = [jnp.broadcast_to(groups[h][:, k + j : k + j + 1], full) for j in range(GROUP)]
            groups[h] = groups[h] - total(cols[j] * steps[j] for j in range(GROUP))
        packed = steps[0]
        for i in range(1, GROUP):
            packed = jnp.where(sub == i, steps[i], packed)
        groups[g] = packed
    return jnp.concatenate([x[:, order:] for x in groups], axis=0)


def invert(work):
    order = work.shape[0]

    def sweep(_, carry):
        head = work[0:BLOCK, :]
        inv = block_inverse(head[:, 0:BLOCK])
        lane = lax.broadcasted_iota(jnp.int32, (BLOCK, order), 1)
        row = lax.broadcasted_iota(jnp.int32, (BLOCK, order), 0)
        band = dot_nn(inv, jnp.where(lane < BLOCK, (lane == row).astype(jnp.float32), head))
        rest = work[BLOCK:order, :]
        lane_low = lax.broadcasted_iota(jnp.int32, (order - BLOCK, order), 1)
        lower = jnp.where(lane_low < BLOCK, 0.0, rest) - dot_nn(rest[:, 0:BLOCK], band)
        work[0 : order - BLOCK, :] = pltpu.roll(lower, order - BLOCK, 1)
        work[order - BLOCK : order, :] = pltpu.roll(band, order - BLOCK, 1)
        return carry

    lax.fori_loop(0, order // BLOCK, sweep, 0)


def diagonal_mask(order):
    return lax.broadcasted_iota(jnp.int32, (order, order), 0) == lax.broadcasted_iota(jnp.int32, (order, order), 1)


def invert_scaled(matrix, work, inverse):
    order = matrix.shape[0]
    diagonal = diagonal_mask(order)
    kept = jnp.where(diagonal, matrix, 0.0)
    row = 1.0 / jnp.sqrt(jnp.sum(kept, axis=0, keepdims=True))
    col = 1.0 / jnp.sqrt(jnp.sum(kept, axis=1, keepdims=True))
    scaled = jnp.where(diagonal, 1.0, matrix * row * col)
    work[...] = scaled
    bound = jnp.max(jnp.sum(jnp.abs(scaled), axis=0, keepdims=True))
    size = jnp.where(bound < 2.0, 1.0, 1.0 / bound)
    inverse[...] = jnp.where(diagonal, 2.0 * size, 0.0) - (size * size) * scaled

    def unfinished(carry):
        residual, step = carry
        return (residual > RESIDUAL) & (step < STEPS)

    def improve(carry):
        step = carry[1]
        guess = inverse[...]
        error = jnp.where(diagonal_mask(order), 1.0, 0.0) - dot_nn(work[...], guess)
        inverse[...] = guess + dot_nn(guess, error)
        return jnp.sum(error * error), step + 1

    carry = (jnp.float32(1.0), jnp.int32(0))
    for _ in range(2):
        carry = improve(carry)
    residual, _ = lax.while_loop(unfinished, improve, carry)

    @pl.when(jnp.logical_not(residual <= RESIDUAL))
    def _():
        invert(work)
        inverse[...] = work[...]

    return row, col


def fetch(tensor_in, tensor, small_in, small, arrived, arrived_small):
    rows = tensor.shape[0] // PARTS

    def copy(i):
        part = pl.ds(i * rows, rows)
        return pltpu.make_async_copy(tensor_in.at[part], tensor.at[part], arrived.at[i])

    copies = [pltpu.make_async_copy(s, t, arrived_small.at[n]) for n, (s, t) in enumerate(zip(small_in, small))]
    for one in copies:
        one.start()
    for i in range(AHEAD):
        copy(i).start()
    for one in copies:
        one.wait()
    for i in range(AHEAD, PARTS):
        copy(i).start()
    return lambda i: copy(i).wait()


def packed_gram(gram):
    low = lax.broadcasted_iota(jnp.int32, (BLOCK, LANES), 1) < BLOCK
    return [
        gram[0:64, 0:128],
        gram[128:192, 0:128],
        gram[192:256, 0:128],
        gram[192:256, 128:256],
        jnp.where(low, gram[128:192, 128:256], gram[64:128, 0:128]),
    ]


def unpacked_gram(slots):
    low = lax.broadcasted_iota(jnp.int32, (BLOCK, LANES), 1) < BLOCK
    none = jnp.zeros((BLOCK, LANES), jnp.float32)
    half = jnp.concatenate(
        [
            jnp.concatenate([slots[0], none], axis=1),
            jnp.concatenate([jnp.where(low, 0.0, slots[4]), none], axis=1),
            jnp.concatenate([slots[1], jnp.where(low, slots[4], 0.0)], axis=1),
            jnp.concatenate([slots[2], slots[3]], axis=1),
        ],
        axis=0,
    )
    shape = half.shape
    row_block = lax.broadcasted_iota(jnp.int32, shape, 0) // BLOCK
    col_block = lax.broadcasted_iota(jnp.int32, shape, 1) // BLOCK
    return half + jnp.where(row_block == col_block, 0.0, half).T


def first_mode_kernel(
    core, tensor_in, factor_b_in, factor_c_in, keep, give, tensor, factor_b, factor_c, arrived, arrived_small, out
):
    x_rows, time_len, depth = tensor.shape
    rank = factor_b.shape[1]
    rows = x_rows // PARTS
    wait_part = fetch(
        tensor_in, tensor, [factor_b_in, factor_c_in], [factor_b, factor_c], arrived, arrived_small
    )
    half = PARTS // CORES
    for t, slot in enumerate(packed_gram(bf16_gram(factor_b[...]))):
        for i in range(PARTS):
            out[i // half, i % half, t * GROUP : (t + 1) * GROUP, :] = slot[i * GROUP : (i + 1) * GROUP]

    def contract(i, carry):
        wait_part(i)
        contracted = jnp.dot(
            tensor[pl.ds(i * rows, rows)].reshape(rows * time_len, depth),
            factor_b[...],
            preferred_element_type=jnp.float32,
        ).reshape(rows, time_len, rank)
        summed = jnp.sum(contracted * factor_c[...].astype(jnp.float32)[None], axis=1)
        for h in range(rank // LANES):
            out[i // half, i % half, pl.ds((SLOTS + h) * GROUP, rows), :] = summed[:, h * LANES : (h + 1) * LANES]
        return carry

    lax.fori_loop(0, PARTS, contract, 0)
    first = core[0] == 0
    keep[...] = jnp.where(first, out[0], out[1])
    give[...] = jnp.where(first, out[1], out[0])


def first_solve_kernel(where, mine, other, factor_c, a_hat, slab, work, inverse, raw):
    rank = work.shape[0]
    share = rank // PARTS
    half = PARTS // CORES
    core = where[0] % CORES
    gathered = [jnp.where(core == p // half, mine[p % half], other[p % half]) for p in range(PARTS)]
    bands = [
        jnp.concatenate([gathered[p][t * GROUP : (t + 1) * GROUP] for p in range(PARTS)], axis=0)
        for t in range(SLOTS + rank // LANES)
    ]
    b_gram = unpacked_gram(bands[:SLOTS])
    m_first = jnp.concatenate(bands[SLOTS:], axis=1)
    row, _ = invert_scaled(b_gram * bf16_gram(factor_c[...]), work, inverse)
    rows = dot_nn(m_first * row, inverse[...]) * row
    a_hat[...] = rows
    raw[...] = dot_tn(rows, rows)
    mine = raw[pl.ds(where[0] * share, share), :]
    squares = jnp.sum(rows * rows, axis=0, keepdims=True)
    for p in range(PARTS):
        top, left = (p // 2) * GROUP, (p % 2) * LANES
        slab[p, 0:GROUP, :] = mine[top : top + GROUP, left : left + LANES]
        slab[p, GROUP:, :] = jnp.zeros((GROUP, LANES), jnp.float32)
        for h in range(rank // LANES):
            slab[p, GROUP + h : GROUP + h + 1, :] = squares[:, h * LANES : (h + 1) * LANES]


def assemble(pieces):
    bands = []
    for q in range(PARTS):
        for p in range(0, PARTS, 2):
            bands.append(jnp.concatenate([pieces[q, p], pieces[q, p + 1]], axis=1))
    return jnp.concatenate(bands, axis=0)


def norm_row(sums):
    squares = total(sums[p, GROUP:, :] for p in range(PARTS))
    return jnp.sqrt(jnp.concatenate([squares[0:1], squares[1:2]], axis=1) + EPSILON)


def second_mode_kernel(
    tensor_in, a_hat_in, sums_in, factor_c_in, out, tensor, a_hat, sums, factor_c, arrived, arrived_small
):
    x_rows, time_len, depth = tensor.shape
    rank = a_hat.shape[1]
    rows, band = JOINED * x_rows // PARTS, depth // PARTS
    wait_part = fetch(
        tensor_in, tensor, [sums_in, a_hat_in, factor_c_in], [sums, a_hat, factor_c], arrived, arrived_small
    )
    norms = norm_row(sums)
    tile = total(sums[p, 0:GROUP, :] for p in range(PARTS))
    for p in range(PARTS):
        out[p, band:, 0:LANES] = tile
        out[p, band:, LANES:] = jnp.zeros((GROUP, rank - LANES), jnp.float32)
    out[:, 0:band, :] = jnp.zeros((PARTS, band, rank), jnp.float32)

    def contract(i, carry):
        for n in range(JOINED):
            wait_part(i * JOINED + n)
        a_unit = a_hat[pl.ds(i * rows, rows), :] / norms
        khatri_rao = (a_unit[:, None, :] * factor_c[...].astype(jnp.float32)[None]).astype(jnp.bfloat16)
        out[:, 0:band, :] += lax.dot_general(
            tensor[pl.ds(i * rows, rows)].reshape(rows * time_len, depth),
            khatri_rao.reshape(rows * time_len, rank),
            (((0,), (0,)), ((), ())),
            preferred_element_type=jnp.float32,
        ).reshape(PARTS, band, rank)
        return carry

    lax.fori_loop(0, PARTS // JOINED, contract, 0)


def second_inverse_kernel(pieces, sums, factor_c, inverse, work):
    raw = assemble(pieces)
    norms = norm_row(sums)
    norms_down = jnp.sum(jnp.where(diagonal_mask(raw.shape[0]), norms, 0.0), axis=1, keepdims=True)
    row, col = invert_scaled(raw * bf16_gram(factor_c[...]), work, inverse)
    inverse[...] = inverse[...] * (row * norms) * (col * norms_down)


def second_solve_kernel(m_second, inverse, b_hat):
    b_hat[...] = dot_nn(total(m_second[p] for p in range(PARTS)), inverse[...])


def f32(*shape):
    return jax.ShapeDtypeStruct(shape, jnp.float32)


def call(kernel, out_shape, *operands, scratch=(), vmem=VMEM_BYTES, **more):
    return pl.pallas_call(
        kernel,
        out_shape=out_shape,
        scratch_shapes=list(scratch),
        compiler_params=pltpu.CompilerParams(vmem_limit_bytes=vmem),
        **more,
    )(*operands)


def stream(kernel, out_shape, *operands, scalars=(), scratch=()):
    return call(
        kernel,
        out_shape,
        *scalars,
        *operands,
        scratch=[
            *(pltpu.VMEM(x.shape, x.dtype) for x in operands),
            pltpu.SemaphoreType.DMA((PARTS,)),
            pltpu.SemaphoreType.DMA((len(operands) - 1,)),
            *scratch,
        ],
        vmem=STREAM_BYTES,
        in_specs=[pl.BlockSpec(memory_space=pltpu.SMEM)] * len(scalars)
        + [pl.BlockSpec(memory_space=pl.ANY)] * len(operands),
    )


def swap_cores(value):
    return lax.ppermute(value, "core", [(0, 1), (1, 0)])


def scatter_sum(parts, axis):
    return jnp.sum(lax.all_to_all(parts, axis, 0, 0), axis=0)


def gather(block, axis, size=PARTS):
    return lax.all_to_all(jnp.broadcast_to(block[None], (size, *block.shape)), axis, 0, 0)


def local(tensor, factor_b, factor_c):
    x_rows, time_len, y_rows = tensor.shape
    rank = factor_b.shape[1]
    square = pltpu.VMEM((rank, rank), jnp.float32)

    whole = pl.BlockSpec(memory_space=pltpu.VMEM)
    where = lax.axis_index(GY).astype(jnp.int32).reshape(1)
    core = lax.axis_index("core").astype(jnp.int32).reshape(1)
    half = f32(PARTS // CORES, (SLOTS + rank // LANES) * GROUP, LANES)
    keep, give = stream(
        first_mode_kernel,
        (half, half),
        tensor,
        factor_b,
        factor_c,
        scalars=[core],
        scratch=[pltpu.VMEM((CORES, *half.shape), jnp.float32)],
    )
    pair = keep + swap_cores(give)
    mine = jnp.sum(gather(pair, "x", PARTS // CORES), axis=0)
    other = swap_cores(mine)

    a_hat, slab = call(
        first_solve_kernel,
        (f32(x_rows, rank), f32(PARTS, 2 * GROUP, LANES)),
        where,
        mine,
        other,
        factor_c,
        scratch=[square, square, square],
        in_specs=[pl.BlockSpec(memory_space=pltpu.SMEM), whole, whole, whole],
    )

    sums = gather(scatter_sum(slab, "gl"), FAR)
    product = stream(
        second_mode_kernel, f32(PARTS, y_rows // PARTS + GROUP, rank), tensor, a_hat, sums, factor_c
    )
    received = lax.all_to_all(product, "gl", 0, 0)
    halves = jnp.sum(received[:, : y_rows // PARTS], axis=0).reshape(HALVES, y_rows // PARTS // HALVES, rank)
    repeated = jnp.broadcast_to(halves[None], (PARTS // HALVES, *halves.shape)).reshape(PARTS, *halves.shape[1:])
    m_second = lax.all_to_all(repeated, FAR, 0, 0)
    pieces = lax.all_gather(received[:, y_rows // PARTS :, :LANES], GY)
    inverse = call(
        second_inverse_kernel, f32(rank, rank), pieces, sums, factor_c, scratch=[square], cost_estimate=INVERSE_COST
    )
    b_band = call(second_solve_kernel, f32(*halves.shape[1:]), m_second, inverse)
    b_hat = gather(b_band, ("gl", "zb"), PARTS * HALVES).reshape(y_rows, rank)
    return (a_hat, b_hat)


def solution(mesh):
    z_and_y = (PARTS // HALVES, HALVES, PARTS)
    split = Mesh(mesh.devices.reshape(*z_and_y, PARTS // CORES, CORES), (*FAR, "gl", *GY))
    x_axes = (*FAR, "gl")
    return jax.shard_map(
        local,
        mesh=split,
        in_specs=(P(x_axes, None, GY), P(GY, None), P()),
        out_specs=(P(x_axes, None), P(GY, None)),
        check_vma=False,
    )
```

```python
import functools

import jax
import jax.numpy as jnp
from jax import lax
from jax.experimental import pallas as pl
from jax.experimental.pallas import tpu as pltpu
from jax.sharding import Mesh
from jax.sharding import PartitionSpec as P

EPSILON = 1e-06
HIGH = lax.Precision.HIGHEST
BLOCK = 64
GROUP = 8
LANES = 128
JOINED = 2
SLOTS = 5
PARTS = 8
HALVES = 2
GY = ("x", "core")
CORES = 2
FAR = ("zh", "zb")
AHEAD = 2
STEPS = 12
RESIDUAL = 1e-8
VMEM_BYTES = 24 * 1024 * 1024
FIRST_BYTES = 107 * 512 * 1024
SECOND_BYTES = 105 * 512 * 1024
INVERSE_COST = pl.CostEstimate(flops=12_000_000_000, bytes_accessed=1_000_000, transcendentals=0)


def dot_nn(left, right):
    return lax.dot_general(left, right, (((1,), (0,)), ((), ())), precision=HIGH, preferred_element_type=jnp.float32)


def dot_tn(left, right):
    return lax.dot_general(left, right, (((0,), (0,)), ((), ())), precision=HIGH, preferred_element_type=jnp.float32)


def bf16_gram(factor):
    return lax.dot_general(factor, factor, (((0,), (0,)), ((), ())), preferred_element_type=jnp.float32)


def total(terms):
    terms = list(terms)
    while len(terms) > 1:
        paired = [terms[i] + terms[i + 1] for i in range(0, len(terms) - 1, 2)]
        terms = paired + ([terms[-1]] if len(terms) % 2 else [])
    return terms[0]


def solve_group(entries, rows):
    n = len(rows)
    e = [list(line) for line in entries]
    rows = list(rows)
    factors, scaled = {}, [None] * n
    for p in range(0, n, 2):
        a, b, c = e[p][p], e[p][p + 1], e[p + 1][p + 1]
        inv_det = pltpu.reciprocal(a * c - b * b, approx=True)
        inv_a, inv_b, inv_c = c * inv_det, b * inv_det, a * inv_det
        for i in range(p + 2, n):
            x, y = e[p][i], e[p + 1][i]
            f0, f1 = inv_a * x - inv_b * y, inv_c * y - inv_b * x
            factors[p, i] = f0, f1
            for j in range(i, n):
                e[i][j] = e[i][j] - (f0 * e[p][j] + f1 * e[p + 1][j])
            rows[i] = rows[i] - (f0 * rows[p] + f1 * rows[p + 1])
        scaled[p] = inv_a * rows[p] - inv_b * rows[p + 1]
        scaled[p + 1] = inv_c * rows[p + 1] - inv_b * rows[p]
    for p in range(n - 4, -1, -2):
        for q in range(2):
            scaled[p + q] = scaled[p + q] - total(factors[p, i][q] * scaled[i] for i in range(p + 2, n))
    return scaled


def block_inverse(block):
    order = block.shape[0]
    width = 2 * order
    count = order // GROUP
    eye = (
        lax.broadcasted_iota(jnp.int32, (order, order), 0) == lax.broadcasted_iota(jnp.int32, (order, order), 1)
    ).astype(jnp.float32)
    wide = jnp.concatenate([block, eye], axis=1)
    groups = [wide[g * GROUP : (g + 1) * GROUP] for g in range(count)]
    sub = lax.broadcasted_iota(jnp.int32, (GROUP, width), 0)
    full = (GROUP, width)
    for g in range(count):
        k = g * GROUP
        rows = [jnp.broadcast_to(groups[g][i : i + 1], full) for i in range(GROUP)]
        entries = [
            [jnp.broadcast_to(rows[i][:, k + j : k + j + 1], full) if j >= i else None for j in range(GROUP)]
            for i in range(GROUP)
        ]
        steps = solve_group(entries, rows)
        order_of = [h for h in range(g + 1, count)] + [h for h in range(g)]
        for h in order_of:
            cols = [jnp.broadcast_to(groups[h][:, k + j : k + j + 1], full) for j in range(GROUP)]
            groups[h] = groups[h] - total(cols[j] * steps[j] for j in range(GROUP))
        packed = steps[0]
        for i in range(1, GROUP):
            packed = jnp.where(sub == i, steps[i], packed)
        groups[g] = packed
    return jnp.concatenate([x[:, order:] for x in groups], axis=0)


def invert(work):
    order = work.shape[0]

    def sweep(_, carry):
        head = work[0:BLOCK, :]
        inv = block_inverse(head[:, 0:BLOCK])
        lane = lax.broadcasted_iota(jnp.int32, (BLOCK, order), 1)
        row = lax.broadcasted_iota(jnp.int32, (BLOCK, order), 0)
        band = dot_nn(inv, jnp.where(lane < BLOCK, (lane == row).astype(jnp.float32), head))
        rest = work[BLOCK:order, :]
        lane_low = lax.broadcasted_iota(jnp.int32, (order - BLOCK, order), 1)
        lower = jnp.where(lane_low < BLOCK, 0.0, rest) - dot_nn(rest[:, 0:BLOCK], band)
        work[0 : order - BLOCK, :] = pltpu.roll(lower, order - BLOCK, 1)
        work[order - BLOCK : order, :] = pltpu.roll(band, order - BLOCK, 1)
        return carry

    lax.fori_loop(0, order // BLOCK, sweep, 0)


def diagonal_mask(order):
    return lax.broadcasted_iota(jnp.int32, (order, order), 0) == lax.broadcasted_iota(jnp.int32, (order, order), 1)


def invert_scaled(matrix, work, inverse):
    order = matrix.shape[0]
    diagonal = diagonal_mask(order)
    kept = jnp.where(diagonal, matrix, 0.0)
    row = 1.0 / jnp.sqrt(jnp.sum(kept, axis=0, keepdims=True))
    col = 1.0 / jnp.sqrt(jnp.sum(kept, axis=1, keepdims=True))
    scaled = jnp.where(diagonal, 1.0, matrix * row * col)
    work[...] = scaled
    bound = jnp.max(jnp.sum(jnp.abs(scaled), axis=0, keepdims=True))
    size = jnp.where(bound < 2.0, 1.0, 1.0 / bound)
    inverse[...] = jnp.where(diagonal, 2.0 * size, 0.0) - (size * size) * scaled

    def unfinished(carry):
        residual, step = carry
        return (residual > RESIDUAL) & (step < STEPS)

    def improve(carry):
        step = carry[1]
        guess = inverse[...]
        error = jnp.where(diagonal_mask(order), 1.0, 0.0) - dot_nn(work[...], guess)
        inverse[...] = guess + dot_nn(guess, error)
        return jnp.sum(error * error), step + 1

    carry = (jnp.float32(1.0), jnp.int32(0))
    for _ in range(2):
        carry = improve(carry)
    residual, _ = lax.while_loop(unfinished, improve, carry)

    @pl.when(jnp.logical_not(residual <= RESIDUAL))
    def _():
        invert(work)
        inverse[...] = work[...]

    return row, col


def fetch(tensor_in, tensor, small_in, small, arrived, arrived_small):
    rows = tensor.shape[0] // PARTS

    def copy(i):
        part = pl.ds(i * rows, rows)
        return pltpu.make_async_copy(tensor_in.at[part], tensor.at[part], arrived.at[i])

    copies = [pltpu.make_async_copy(s, t, arrived_small.at[n]) for n, (s, t) in enumerate(zip(small_in, small))]
    for one in copies:
        one.start()
    for i in range(AHEAD):
        copy(i).start()
    for one in copies:
        one.wait()
    for i in range(AHEAD, PARTS):
        copy(i).start()
    return lambda i: copy(i).wait()


def packed_gram(gram):
    low = lax.broadcasted_iota(jnp.int32, (BLOCK, LANES), 1) < BLOCK
    return [
        gram[0:64, 0:128],
        gram[128:192, 0:128],
        gram[192:256, 0:128],
        gram[192:256, 128:256],
        jnp.where(low, gram[128:192, 128:256], gram[64:128, 0:128]),
    ]


def unpacked_gram(slots):
    low = lax.broadcasted_iota(jnp.int32, (BLOCK, LANES), 1) < BLOCK
    none = jnp.zeros((BLOCK, LANES), jnp.float32)
    half = jnp.concatenate(
        [
            jnp.concatenate([slots[0], none], axis=1),
            jnp.concatenate([jnp.where(low, 0.0, slots[4]), none], axis=1),
            jnp.concatenate([slots[1], jnp.where(low, slots[4], 0.0)], axis=1),
            jnp.concatenate([slots[2], slots[3]], axis=1),
        ],
        axis=0,
    )
    shape = half.shape
    row_block = lax.broadcasted_iota(jnp.int32, shape, 0) // BLOCK
    col_block = lax.broadcasted_iota(jnp.int32, shape, 1) // BLOCK
    return half + jnp.where(row_block == col_block, 0.0, half).T


def first_mode_kernel(
    core, tensor_in, factor_b_in, factor_c_in, keep, give, tensor, factor_b, factor_c, arrived, arrived_small, out
):
    x_rows, time_len, depth = tensor.shape
    rank = factor_b.shape[1]
    rows = x_rows // PARTS
    wait_part = fetch(
        tensor_in, tensor, [factor_b_in, factor_c_in], [factor_b, factor_c], arrived, arrived_small
    )
    half = PARTS // CORES
    for t, slot in enumerate(packed_gram(bf16_gram(factor_b[...]))):
        for i in range(PARTS):
            out[i // half, i % half, t * GROUP : (t + 1) * GROUP, :] = slot[i * GROUP : (i + 1) * GROUP]

    def contract(i, carry):
        wait_part(i)
        contracted = jnp.dot(
            tensor[pl.ds(i * rows, rows)].reshape(rows * time_len, depth),
            factor_b[...],
            preferred_element_type=jnp.float32,
        ).reshape(rows, time_len, rank)
        summed = jnp.sum(contracted * factor_c[...].astype(jnp.float32)[None], axis=1)
        for h in range(rank // LANES):
            out[i // half, i % half, pl.ds((SLOTS + h) * GROUP, rows), :] = summed[:, h * LANES : (h + 1) * LANES]
        return carry

    lax.fori_loop(0, PARTS, contract, 0)
    first = core[0] == 0
    keep[...] = jnp.where(first, out[0], out[1])
    give[...] = jnp.where(first, out[1], out[0])


def first_solve_kernel(where, mine, other, factor_c, a_hat, a_near, slab, work, inverse, raw):
    rank = work.shape[0]
    share = rank // PARTS
    half = PARTS // CORES
    core = where[0] % CORES
    gathered = [jnp.where(core == p // half, mine[p % half], other[p % half]) for p in range(PARTS)]
    bands = [
        jnp.concatenate([gathered[p][t * GROUP : (t + 1) * GROUP] for p in range(PARTS)], axis=0)
        for t in range(SLOTS + rank // LANES)
    ]
    b_gram = unpacked_gram(bands[:SLOTS])
    m_first = jnp.concatenate(bands[SLOTS:], axis=1)
    row, _ = invert_scaled(b_gram * bf16_gram(factor_c[...]), work, inverse)
    rows = dot_nn(m_first * row, inverse[...]) * row
    a_hat[...] = rows
    a_near[...] = rows
    raw[...] = dot_tn(rows, rows)
    mine = raw[pl.ds(where[0] * share, share), :]
    squares = jnp.sum(rows * rows, axis=0, keepdims=True)
    for p in range(PARTS):
        top, left = (p // 2) * GROUP, (p % 2) * LANES
        slab[p, 0:GROUP, :] = mine[top : top + GROUP, left : left + LANES]
        slab[p, GROUP:, :] = jnp.zeros((GROUP, LANES), jnp.float32)
        for h in range(rank // LANES):
            slab[p, GROUP + h : GROUP + h + 1, :] = squares[:, h * LANES : (h + 1) * LANES]


def assemble(pieces):
    bands = []
    for q in range(PARTS):
        for p in range(0, PARTS, 2):
            bands.append(jnp.concatenate([pieces[q, p], pieces[q, p + 1]], axis=1))
    return jnp.concatenate(bands, axis=0)


def norm_row(sums):
    squares = total(sums[p, GROUP:, :] for p in range(PARTS))
    return jnp.sqrt(jnp.concatenate([squares[0:1], squares[1:2]], axis=1) + EPSILON)


def second_mode_kernel(
    tensor_in, a_hat_in, sums_in, factor_c_in, out, tensor, a_hat, sums, factor_c, arrived, arrived_small
):
    x_rows, time_len, depth = tensor.shape
    rank = a_hat.shape[1]
    rows, band = JOINED * x_rows // PARTS, depth // PARTS
    wait_part = fetch(
        tensor_in, tensor, [sums_in, a_hat_in, factor_c_in], [sums, a_hat, factor_c], arrived, arrived_small
    )
    norms = norm_row(sums)
    tile = total(sums[p, 0:GROUP, :] for p in range(PARTS))
    for p in range(PARTS):
        out[p, band:, 0:LANES] = tile
        out[p, band:, LANES:] = jnp.zeros((GROUP, rank - LANES), jnp.float32)
    out[:, 0:band, :] = jnp.zeros((PARTS, band, rank), jnp.float32)

    def contract(i, carry):
        for n in range(JOINED):
            wait_part(i * JOINED + n)
        a_unit = a_hat[pl.ds(i * rows, rows), :] / norms
        khatri_rao = (a_unit[:, None, :] * factor_c[...].astype(jnp.float32)[None]).astype(jnp.bfloat16)
        out[:, 0:band, :] += lax.dot_general(
            tensor[pl.ds(i * rows, rows)].reshape(rows * time_len, depth),
            khatri_rao.reshape(rows * time_len, rank),
            (((0,), (0,)), ((), ())),
            preferred_element_type=jnp.float32,
        ).reshape(PARTS, band, rank)
        return carry

    lax.fori_loop(0, PARTS // JOINED, contract, 0)


def second_inverse_kernel(pieces, sums, factor_c, inverse, work):
    raw = assemble(pieces)
    norms = norm_row(sums)
    norms_down = jnp.sum(jnp.where(diagonal_mask(raw.shape[0]), norms, 0.0), axis=1, keepdims=True)
    row, col = invert_scaled(raw * bf16_gram(factor_c[...]), work, inverse)
    inverse[...] = inverse[...] * (row * norms) * (col * norms_down)


def second_solve_kernel(m_second, inverse, b_hat):
    b_hat[...] = dot_nn(total(m_second[p] for p in range(PARTS)), inverse[...])


def f32(*shape):
    return jax.ShapeDtypeStruct(shape, jnp.float32)


def call(kernel, out_shape, *operands, scratch=(), vmem=VMEM_BYTES, **more):
    return pl.pallas_call(
        kernel,
        out_shape=out_shape,
        scratch_shapes=list(scratch),
        compiler_params=pltpu.CompilerParams(vmem_limit_bytes=vmem),
        **more,
    )(*operands)


def stream(kernel, out_shape, *operands, vmem, scalars=(), scratch=()):
    return call(
        kernel,
        out_shape,
        *scalars,
        *operands,
        scratch=[
            *(pltpu.VMEM(x.shape, x.dtype) for x in operands),
            pltpu.SemaphoreType.DMA((PARTS,)),
            pltpu.SemaphoreType.DMA((len(operands) - 1,)),
            *scratch,
        ],
        vmem=vmem,
        in_specs=[pl.BlockSpec(memory_space=pltpu.SMEM)] * len(scalars)
        + [pl.BlockSpec(memory_space=pl.ANY)] * len(operands),
    )


def swap_cores(value):
    return lax.ppermute(value, "core", [(0, 1), (1, 0)])


def scatter_sum(parts, axis):
    return jnp.sum(lax.all_to_all(parts, axis, 0, 0), axis=0)


def gather(block, axis, size=PARTS):
    return lax.all_to_all(jnp.broadcast_to(block[None], (size, *block.shape)), axis, 0, 0)


def local(tensor, factor_b, factor_c):
    x_rows, time_len, y_rows = tensor.shape
    rank = factor_b.shape[1]
    square = pltpu.VMEM((rank, rank), jnp.float32)

    whole = pl.BlockSpec(memory_space=pltpu.VMEM)
    where = lax.axis_index(GY).astype(jnp.int32).reshape(1)
    core = lax.axis_index("core").astype(jnp.int32).reshape(1)
    half = f32(PARTS // CORES, (SLOTS + rank // LANES) * GROUP, LANES)
    keep, give = stream(
        first_mode_kernel,
        (half, half),
        tensor,
        factor_b,
        factor_c,
        vmem=FIRST_BYTES,
        scalars=[core],
        scratch=[pltpu.VMEM((CORES, *half.shape), jnp.float32)],
    )
    pair = keep + swap_cores(give)
    mine = jnp.sum(gather(pair, "x", PARTS // CORES), axis=0)
    other = swap_cores(mine)

    a_hat, a_near, slab = call(
        first_solve_kernel,
        (f32(x_rows, rank), f32(x_rows, rank), f32(PARTS, 2 * GROUP, LANES)),
        where,
        mine,
        other,
        factor_c,
        scratch=[square, square, square],
        in_specs=[pl.BlockSpec(memory_space=pltpu.SMEM), whole, whole, whole],
    )

    sums = gather(scatter_sum(slab, "gl"), FAR)
    product = stream(
        second_mode_kernel,
        f32(PARTS, y_rows // PARTS + GROUP, rank),
        tensor,
        a_near,
        sums,
        factor_c,
        vmem=SECOND_BYTES,
    )
    received = lax.all_to_all(product, "gl", 0, 0)
    halves = jnp.sum(received[:, : y_rows // PARTS], axis=0).reshape(HALVES, y_rows // PARTS // HALVES, rank)
    repeated = jnp.broadcast_to(halves[None], (PARTS // HALVES, *halves.shape)).reshape(PARTS, *halves.shape[1:])
    m_second = lax.all_to_all(repeated, FAR, 0, 0)
    pieces = lax.all_gather(received[:, y_rows // PARTS :, :LANES], GY)
    inverse = call(
        second_inverse_kernel, f32(rank, rank), pieces, sums, factor_c, scratch=[square], cost_estimate=INVERSE_COST
    )
    b_band = call(second_solve_kernel, f32(*halves.shape[1:]), m_second, inverse)
    b_hat = gather(b_band, ("gl", "zb"), PARTS * HALVES).reshape(y_rows, rank)
    return (a_hat, b_hat)


def solution(mesh):
    z_and_y = (PARTS // HALVES, HALVES, PARTS)
    split = Mesh(mesh.devices.reshape(*z_and_y, PARTS // CORES, CORES), (*FAR, "gl", *GY))
    x_axes = (*FAR, "gl")
    return jax.shard_map(
        local,
        mesh=split,
        in_specs=(P(x_axes, None, GY), P(GY, None), P()),
        out_specs=(P(x_axes, None), P(GY, None)),
        check_vma=False,
    )
```
